128 devices in a mesh: ctx: 16 (over x, z), dp: 8 (over y, core).
Axes of the slice: x: 4, y: 4, z: 4, core: 2. Of those that a mesh axis runs over, the one named last changes fastest.
Arguments:
- queries: bfloat16 [8, 8192, 2048], P('dp', 'ctx'), may hold values from -6 to 6
- keys: bfloat16 [8, 8192, 2048], P('dp', 'ctx'), may hold values from -6 to 6
- values: bfloat16 [8, 8192, 2048], P('dp', 'ctx'), may hold values from -6 to 6
- out_weight: bfloat16 [2048, 2048], replicated, may hold values from -0.125 to 0.125
- out_grad: bfloat16 [8, 8192, 2048], P('dp', 'ctx'), may hold values from -6 to 6
Outputs:
- attended: bfloat16 [8, 8192, 2048], P('dp', 'ctx')
- query_grad: bfloat16 [8, 8192, 2048], P('dp', 'ctx')
- key_grad: bfloat16 [8, 8192, 2048], P('dp', 'ctx')
- value_grad: bfloat16 [8, 8192, 2048], P('dp', 'ctx')
- weight_grad: float32 [2048, 2048], P(('ctx', 'dp'))
The draws below stay inside these ranges and needn't reach their ends.
All inputs are finite; a program needn't handle non-finite values.
Results may differ from the reference program's by a relative error of at most 0.02.
Values may be sent and summed in bfloat16 or wider, within the bound.
A program may use at most 192 MiB of HBM per device.

```python
import jax
import jax.numpy as jnp
from jax import lax

H = 16
DK = 128
DOUT = 2048
TOK_DEV = 512
LENGTH = 8192
SEQS = 8


def shard_levels(stream_key, extent, shards, low, high):
    def one(position, parts):
        draws = jax.random.uniform(jax.random.fold_in(jax.random.fold_in(stream_key, 6), position), (parts,), jnp.float32, low / len(shards), high / len(shards))
        return jnp.repeat(jnp.exp(draws), extent[position] // parts).reshape((-1,) + (1,) * (len(extent) - position - 1))

    loudness = one(*shards[0])
    for cut in shards[1:]:
        loudness = loudness * one(*cut)
    return loudness


def centred(stream_key, extent, width, bound, shards=(), kind=jnp.bfloat16):
    factor_of = shard_levels(stream_key, extent, shards, -0.22, 0.18) if shards else 1.0
    result = jax.random.normal(stream_key, extent, jnp.float32) * width * factor_of
    return jnp.minimum(jnp.maximum(result, -bound), bound).astype(kind)


def setup_inputs(seed: int = 0) -> dict:
    arg_keys = jax.random.split(jax.random.key(seed), 6)
    queries = centred(arg_keys[0], (SEQS, LENGTH, H * DK), 1.0, 6.0, ((0, 8), (1, 16)))
    keys = centred(arg_keys[1], (SEQS, LENGTH, H * DK), 1.0, 6.0, ((0, 8), (1, 16)))
    values = centred(arg_keys[2], (SEQS, LENGTH, H * DK), 1.0, 6.0, ((0, 8), (1, 16)))
    out_weight = centred(arg_keys[3], (H * DK, DOUT), (H * DK) ** -0.5, 0.125)
    out_grad = centred(arg_keys[4], (SEQS, LENGTH, DOUT), 1.0, 6.0, ((0, 8), (1, 16)))
    return {"queries": queries, "keys": keys, "values": values, "out_weight": out_weight, "out_grad": out_grad}


def block_terms(blocks):
    query_blk, key_blk, value_blk, scaled_blk, factor_blk, before_blk, after_blk = blocks
    query_f = query_blk.astype(jnp.float32)
    key_f = key_blk.astype(jnp.float32)
    value_f = value_blk.astype(jnp.float32)
    scaled_f = scaled_blk.astype(jnp.float32)
    before_f = before_blk.astype(jnp.float32)
    after_f = after_blk.astype(jnp.float32)
    tok_rows = query_blk.shape[0]
    row_ids = jnp.arange(tok_rows, dtype=jnp.int32)
    causal = row_ids[:, None] >= row_ids[None, :]
    scores = jnp.einsum('thd,shd->hts', query_f, key_f)
    weights = jnp.where(causal[None], scores, 0.0).astype(jnp.bfloat16).astype(jnp.float32)
    inner = jnp.einsum('hts,she->the', weights, value_f) + jnp.einsum('thd,hde->the', query_f, before_f)
    attended = (factor_blk * inner).astype(jnp.bfloat16)
    mixing = jnp.einsum('the,she->hts', scaled_f, value_f)
    mixing = jnp.where(causal[None], mixing, 0.0).astype(jnp.bfloat16).astype(jnp.float32)
    query_grad = jnp.einsum('hts,shd->thd', mixing, key_f) + jnp.einsum('the,hde->thd', scaled_f, before_f)
    key_grad = jnp.einsum('hts,thd->shd', mixing, query_f) + jnp.einsum('she,hde->shd', value_f, after_f)
    value_grad = jnp.einsum('hts,the->she', weights, scaled_f) + jnp.einsum('shd,hde->she', key_f, after_f)
    return (attended, query_grad.astype(jnp.bfloat16), key_grad.astype(jnp.bfloat16), value_grad.astype(jnp.bfloat16))

def reference(queries, keys, values, out_weight, out_grad):
    seq_count, total, feature_width = queries.shape
    head_count = feature_width // DK
    block_count = total // TOK_DEV
    positions = jnp.arange(total, dtype=jnp.int32)
    factor = lax.rsqrt(((positions + 1) * DK).astype(jnp.float32)).reshape(block_count, TOK_DEV, 1, 1)
    weight_sum = jnp.zeros((feature_width, out_weight.shape[1]), jnp.float32)
    results = []
    for sequence in range(seq_count):

        def split(array):
            return array.reshape(block_count, TOK_DEV, head_count, DK)
        query_b = split(queries[sequence])
        key_b = split(keys[sequence])
        value_b = split(values[sequence])
        grad_out = jnp.dot(out_grad[sequence], out_weight.T, preferred_element_type=jnp.float32).astype(jnp.bfloat16)
        scaled = (split(grad_out).astype(jnp.float32) * factor).astype(jnp.bfloat16)
        kv_state = jnp.einsum('bthd,bthe->bhde', key_b.astype(jnp.float32), value_b.astype(jnp.float32)).astype(jnp.bfloat16)
        grad_state = jnp.einsum('bthd,bthe->bhde', query_b.astype(jnp.float32), scaled.astype(jnp.float32)).astype(jnp.bfloat16)
        empty_state = jnp.zeros((1, head_count, DK, DK), jnp.float32)
        run_fwd = jnp.cumsum(kv_state.astype(jnp.float32), axis=0)
        before = jnp.concatenate([empty_state, run_fwd[:-1]], axis=0).astype(jnp.bfloat16)
        run_bwd = jnp.flip(jnp.cumsum(jnp.flip(grad_state.astype(jnp.float32), 0), axis=0), 0)
        after = jnp.concatenate([run_bwd[1:], empty_state], axis=0).astype(jnp.bfloat16)
        pieces = lax.map(block_terms, (query_b, key_b, value_b, scaled, factor, before, after))
        merged = [piece.reshape(total, feature_width) for piece in pieces]
        weight_sum = weight_sum + jnp.dot(merged[0].T, out_grad[sequence], preferred_element_type=jnp.float32)
        results.append(merged)
    grad_scale = 1.0 / jnp.sqrt(jnp.float32(seq_count * total))
    weight_grad = weight_sum * grad_scale
    attended = jnp.stack([item[0] for item in results])
    query_grad = jnp.stack([item[1] for item in results])
    key_grad = jnp.stack([item[2] for item in results])
    value_grad = jnp.stack([item[3] for item in results])
    return (attended, query_grad, key_grad, value_grad, weight_grad)
```

```python
import functools
import math

import jax
import jax.numpy as jnp
from jax import lax
from jax.experimental import pallas as pl
from jax.experimental.pallas import tpu as pltpu
from jax.sharding import PartitionSpec as P

DK = 128
CH = 256
MESH = pl.DeviceIdType.MESH
BF = jnp.bfloat16
F32 = jnp.float32
PIECES = (
    (0, 384, "yxz"),
    (384, 384, "xzy"),
    (768, 384, "zyx"),
    (1152, 384, "yzx"),
    (1536, 256, "xyz"),
    (1792, 256, "zxy"),
)
AXES = "xzy"


def dot_nn(a, b):
    return lax.dot_general(a, b, (((1,), (0,)), ((), ())), preferred_element_type=F32)


def dot_nt(a, b):
    return lax.dot_general(a, b, (((1,), (1,)), ((), ())), preferred_element_type=F32)


def dot_tn(a, b):
    return lax.dot_general(a, b, (((0,), (0,)), ((), ())), preferred_element_type=F32)


def head_cols(h):
    return pl.ds(pl.multiple_of(h * DK, DK), DK)


def causal_mask():
    rows = lax.broadcasted_iota(jnp.int32, (CH, CH), 0)
    cols = lax.broadcasted_iota(jnp.int32, (CH, CH), 1)
    return rows >= cols


def token_factor(me, first, rows):
    pos = me * 512 + first + lax.broadcasted_iota(jnp.int32, (rows, DK), 0)
    return lax.rsqrt(((pos + 1) * DK).astype(F32))


def main_kernel(
    grad_scale,
    q_hbm, k_hbm, v_hbm, w_hbm, og_hbm,
    att_hbm, scaled_hbm, before_hbm, after_hbm, wgrad_hbm,
    qb, kb, vb, wb, ogb, og_mate, scaled, inner, att, att_t, mate_t,
    s1, tx_kv, rx_kv, px_kv, before, tx_g, rx_g, px_g, after, wgrad,
    prod, rx1, sum1, rx2, sum2, rx3,
    in_sem, out_sem, og_sem, kv1_s, kv1_r, kv2_s, kv2_r, g1_s, g1_r, g2_s, g2_r,
    mate_s, mate_r, rs_s, rs_r,
):
    me = lax.axis_index("ctx")
    dp = lax.axis_index("dp")
    place = {"x": me // 4, "z": me % 4, "y": dp // 2}
    core = dp % 2
    mate = (me, (dp // 2) * 2 + (1 - core))
    count = 16

    def axis_peer(axis, offset):
        at = dict(place)
        at[axis] = (place[axis] + offset) % 4
        return (at["x"] * 4 + at["z"], at["y"] * 2 + core)

    loads = [
        pltpu.make_async_copy(src.at[0], dst, in_sem.at[n])
        for n, (src, dst) in enumerate(((k_hbm, kb), (v_hbm, vb), (og_hbm, ogb), (q_hbm, qb)))
    ]
    loads.append(pltpu.make_async_copy(w_hbm, wb, in_sem.at[4]))
    loads[0].start()
    loads[1].start()
    loads[2].start()
    loads[4].start()
    loads[3].start()

    barrier = pltpu.get_barrier_semaphore()
    for offset in range(1, count):
        pl.semaphore_signal(
            barrier, inc=1, device_id=((me + offset) % count, dp), device_id_type=MESH
        )
    pl.semaphore_signal(barrier, inc=1, device_id=mate, device_id_type=MESH)
    for offset in range(1, 4):
        pl.semaphore_signal(
            barrier, inc=1, device_id=axis_peer("y", offset), device_id_type=MESH
        )

    loads[0].wait()
    loads[1].wait()

    def kv_one(h, carry):
        cols = head_cols(h)
        first = dot_tn(kb[0:CH, cols], vb[0:CH, cols])
        second = dot_tn(kb[CH : 2 * CH, cols], vb[CH : 2 * CH, cols])
        s1[h] = first.astype(BF)
        tx_kv[h] = (first + second).astype(BF)
        return carry

    lax.fori_loop(0, count, kv_one, 0)
    rx_kv[me] = tx_kv[me]
    pl.semaphore_wait(barrier, count - 1 + 1 + 3)

    def exchange(src, dst, send, recv, offset):
        other = (me + offset) % count
        return pltpu.make_async_remote_copy(
            src_ref=src.at[other], dst_ref=dst.at[me], send_sem=send.at[other],
            recv_sem=recv.at[me], device_id=(other, dp), device_id_type=MESH,
        )

    def arrival(src, dst, send, recv, other):
        return pltpu.make_async_remote_copy(
            src_ref=src.at[other], dst_ref=dst.at[other], send_sem=send.at[other],
            recv_sem=recv.at[other], device_id=(other, dp), device_id_type=MESH,
        )

    def send_all(src, dst, send, recv):
        def one(offset, carry):
            exchange(src, dst, send, recv, offset).start()
            return carry

        lax.fori_loop(1, count, one, 0)

    send_all(tx_kv, rx_kv, kv1_s, kv1_r)

    loads[2].wait()
    og_copy = pltpu.make_async_remote_copy(
        src_ref=ogb, dst_ref=og_mate, send_sem=og_sem.at[0], recv_sem=og_sem.at[1],
        device_id=mate, device_id_type=MESH,
    )
    og_copy.start()

    loads[4].wait()
    loads[3].wait()

    def grad_one(j, carry):
        wide = pl.ds(pl.multiple_of(j * 256, 256), 256)
        grad_out = dot_nt(ogb[...], wb[wide, :]).astype(BF).astype(F32)
        factor = token_factor(me, 0, 512)
        for n in range(2):
            cols = head_cols(2 * j + n)
            here = (grad_out[:, n * DK : (n + 1) * DK] * factor).astype(BF)
            scaled[:, cols] = here
            tx_g[2 * j + n] = dot_tn(qb[:, cols], here).astype(BF)
        return carry

    lax.fori_loop(0, count // 2, grad_one, 0)
    scaled_out = pltpu.make_async_copy(scaled, scaled_hbm, out_sem.at[0])
    scaled_out.start()
    rx_g[me] = tx_g[me]
    send_all(tx_g, rx_g, g1_s, g1_r)

    def scan(src, dst, send, recv, src2, dst2, send2, recv2, reverse):
        def one(n, total):
            b = count - 1 - n if reverse else n

            @pl.when(b != me)
            def _():
                arrival(src, dst, send, recv, b).wait_recv()

            src2[b] = total.astype(BF)

            @pl.when(b != me)
            def _():
                pltpu.make_async_remote_copy(
                    src_ref=src2.at[b], dst_ref=dst2.at[me], send_sem=send2.at[b],
                    recv_sem=recv2.at[me], device_id=(b, dp), device_id_type=MESH,
                ).start()

            return total + dst[b].astype(F32)

        lax.fori_loop(0, count, one, jnp.zeros((DK, DK), F32))
        dst2[me] = src2[me]

    def finish(src, dst, send, recv, which):
        def one(offset, carry):
            other = (me + offset) % count
            if which == "recv":
                arrival(src, dst, send, recv, other).wait_recv()
            else:
                arrival(src, dst, send, recv, other).wait_send()
            return carry

        lax.fori_loop(1, count, one, 0)

    scan(tx_kv, rx_kv, kv1_s, kv1_r, px_kv, before, kv2_s, kv2_r, False)

    def inner_one(h, carry):
        cols = head_cols(h)
        mask = causal_mask()
        for c in range(2):
            rows = pl.ds(c * CH, CH)
            weights = jnp.where(mask, dot_nt(qb[rows, cols], kb[rows, cols]), 0.0).astype(BF)
            part = dot_nn(weights, vb[rows, cols])
            if c == 1:
                part = part + dot_nn(qb[rows, cols], s1[h])
            inner[rows, cols] = part
        return carry

    lax.fori_loop(0, count, inner_one, 0)

    scan(tx_g, rx_g, g1_s, g1_r, px_g, after, g2_s, g2_r, True)

    finish(px_kv, before, kv2_s, kv2_r, "recv")
    before_out = pltpu.make_async_copy(before, before_hbm, out_sem.at[1])
    before_out.start()

    def mate_copy(h):
        return pltpu.make_async_remote_copy(
            src_ref=att_t.at[1 - core, h], dst_ref=mate_t.at[h], send_sem=mate_s.at[h],
            recv_sem=mate_r.at[h], device_id=mate, device_id_type=MESH,
        )

    def att_one(h, carry):
        cols = head_cols(h)
        for c in range(2):
            rows = pl.ds(c * CH, CH)
            total = inner[rows, cols] + dot_nn(qb[rows, cols], before[h])
            total = total * token_factor(me, c * CH, CH)
            att[rows, cols] = total.astype(BF)
            turned = total.T.astype(BF)
            for y in range(4):
                for n in range(2):
                    first = y * 32 + n * 16
                    att_t[n, h, y, :, c * CH : (c + 1) * CH] = turned[first : first + 16]
        mate_copy(h).start()
        return carry

    lax.fori_loop(0, count, att_one, 0)
    att_out = pltpu.make_async_copy(att, att_hbm, out_sem.at[2])
    att_out.start()

    og_copy.wait()

    def mate_wait(h, carry):
        mate_copy(h).wait()
        return carry

    lax.fori_loop(0, count, mate_wait, 0)

    def pick(ref, axes, axis, t):
        index = tuple(t if a == axis else slice(None) for a in axes)
        return ref.at[index]

    def rs_copy(p, phase, offset):
        first, width, order = PIECES[p]
        axes = [a for a in AXES if a not in order[:phase]]
        axis = order[phase]
        src = (prod, sum1, sum2)[phase][p]
        dst = (rx1, rx2, rx3)[phase][p]
        return pltpu.make_async_remote_copy(
            src_ref=pick(src, axes, axis, (place[axis] + offset) % 4),
            dst_ref=dst.at[offset - 1],
            send_sem=rs_s.at[phase, p, offset - 1],
            recv_sem=rs_r.at[phase, p, offset - 1],
            device_id=axis_peer(axis, offset), device_id_type=MESH,
        )

    def rs_sum(p, phase):
        first, width, order = PIECES[p]
        axes = [a for a in AXES if a not in order[:phase]]
        axis = order[phase]
        for offset in range(1, 4):
            rs_copy(p, phase, offset).wait_recv()
        src = (prod, sum1, sum2)[phase][p]
        dst = (rx1, rx2, rx3)[phase][p]
        total = pick(src, axes, axis, place[axis])[...].astype(F32)
        for n in range(3):
            total = total + dst[n].astype(F32)
        return total

    for p, (first, width, order) in enumerate(PIECES):
        def prod_half(n, carry, p=p, first=first, width=width):
            rows = pl.ds(n * 8, 8)
            left = att_t[core, rows].reshape(512, 512)
            part = dot_nn(left, ogb[:, first : first + width])
            other = mate_t[rows].reshape(512, 512)
            part = part + dot_nn(other, og_mate[:, first : first + width])
            prod[p][pl.ds(n * 2, 2)] = part.astype(BF).reshape(2, 4, 4, 16, width)
            return carry

        lax.fori_loop(0, 2, prod_half, 0)
        for offset in range(1, 4):
            rs_copy(p, 0, offset).start()

    finish(px_g, after, g2_s, g2_r, "recv")
    after_out = pltpu.make_async_copy(after, after_hbm, out_sem.at[3])
    after_out.start()

    for p in range(len(PIECES)):
        sum1[p][...] = rs_sum(p, 0).astype(BF)
        for offset in range(1, 4):
            rs_copy(p, 1, offset).start()
    for p in range(len(PIECES)):
        sum2[p][...] = rs_sum(p, 1).astype(BF)
        for offset in range(1, 4):
            rs_copy(p, 2, offset).start()
    for p, (first, width, order) in enumerate(PIECES):
        wgrad[:, first : first + width] = rs_sum(p, 2) * grad_scale
    wgrad_out = pltpu.make_async_copy(wgrad, wgrad_hbm, out_sem.at[4])
    wgrad_out.start()

    finish(tx_kv, rx_kv, kv1_s, kv1_r, "send")
    finish(tx_g, rx_g, g1_s, g1_r, "send")
    finish(px_kv, before, kv2_s, kv2_r, "send")
    finish(px_g, after, g2_s, g2_r, "send")
    for p in range(len(PIECES)):
        for phase in range(3):
            for offset in range(1, 4):
                rs_copy(p, phase, offset).wait_send()
    scaled_out.wait()
    before_out.wait()
    att_out.wait()
    after_out.wait()
    wgrad_out.wait()


def main_call(q, k, v, w, og, grad_scale):
    any_spec = pl.BlockSpec(memory_space=pl.ANY)
    n = len(PIECES)
    widths = [width for _, width, _ in PIECES]
    vm = pltpu.VMEM
    sem = pltpu.SemaphoreType.DMA
    state = vm((16, DK, DK), BF)
    scratch = [
        vm((512, 2048), BF), vm((512, 2048), BF), vm((512, 2048), BF), vm((2048, 2048), BF),
        vm((512, 2048), BF), vm((512, 2048), BF), vm((512, 2048), BF), vm((512, 2048), F32),
        vm((512, 2048), BF), vm((2, 16, 4, 16, 512), BF), vm((16, 4, 16, 512), BF),
        state, state, state, state, state, state, state, state, state, vm((16, 2048), F32),
        [vm((4, 4, 4, 16, c), BF) for c in widths],
        [vm((3, 4, 4, 16, c), BF) for c in widths],
        [vm((4, 4, 16, c), BF) for c in widths],
        [vm((3, 4, 16, c), BF) for c in widths],
        [vm((4, 16, c), BF) for c in widths],
        [vm((3, 16, c), BF) for c in widths],
        sem((5,)), sem((5,)), sem((2,)),
        sem((16,)), sem((16,)), sem((16,)), sem((16,)),
        sem((16,)), sem((16,)), sem((16,)), sem((16,)),
        sem((16,)), sem((16,)), sem((3, n, 3)), sem((3, n, 3)),
    ]
    return pl.pallas_call(
        functools.partial(main_kernel, grad_scale),
        out_shape=(
            jax.ShapeDtypeStruct((512, 2048), BF),
            jax.ShapeDtypeStruct((512, 2048), BF),
            jax.ShapeDtypeStruct((16, DK, DK), BF),
            jax.ShapeDtypeStruct((16, DK, DK), BF),
            jax.ShapeDtypeStruct((16, 2048), F32),
        ),
        in_specs=[any_spec] * 5,
        out_specs=(any_spec,) * 5,
        scratch_shapes=scratch,
        compiler_params=pltpu.CompilerParams(
            collective_id=1, has_side_effects=True, vmem_limit_bytes=56 << 20
        ),
        name="states_and_weight_grad",
    )(q, k, v, w, og)


def grads_kernel(q, k, v, s, before, after, att_hbm, qg, kg, vg, att_out, sem):
    step = pl.program_id(0)
    copy = pltpu.make_async_copy(att_hbm, att_out.at[0], sem)

    @pl.when(step == 0)
    def _():
        copy.start()

    mask = causal_mask()
    low, high = slice(0, CH), slice(CH, 2 * CH)
    for n in range(2):
        cols = slice(n * DK, (n + 1) * DK)
        early = dot_tn(k[0, low, cols], v[0, low, cols])
        late = dot_tn(q[0, high, cols], s[high, cols])
        before_of = (before[n], (before[n].astype(F32) + early).astype(BF))
        after_of = ((after[n].astype(F32) + late).astype(BF), after[n])
        for c, rows in enumerate((low, high)):
            qc, kc, vc, sc = q[0, rows, cols], k[0, rows, cols], v[0, rows, cols], s[rows, cols]
            weights = jnp.where(mask, dot_nt(qc, kc), 0.0).astype(BF)
            mixing = jnp.where(mask, dot_nt(sc, vc), 0.0).astype(BF)
            qg[0, rows, cols] = (dot_nn(mixing, kc) + dot_nt(sc, before_of[c])).astype(BF)
            kg[0, rows, cols] = (dot_tn(mixing, qc) + dot_nt(vc, after_of[c])).astype(BF)
            vg[0, rows, cols] = (dot_tn(weights, sc) + dot_nn(kc, after_of[c])).astype(BF)

    @pl.when(step == pl.num_programs(0) - 1)
    def _():
        copy.wait()


def grads_call(q, k, v, s, before, after, att):
    big = pl.BlockSpec((1, 512, 256), lambda j: (0, 0, j))
    flat = pl.BlockSpec((512, 256), lambda j: (0, j))
    state = pl.BlockSpec((2, DK, DK), lambda j: (j, 0, 0))
    any_spec = pl.BlockSpec(memory_space=pl.ANY)
    shape = jax.ShapeDtypeStruct((1, 512, 2048), BF)
    return pl.pallas_call(
        grads_kernel,
        grid=(8,),
        out_shape=(shape,) * 4,
        in_specs=[big, big, big, flat, state, state, any_spec],
        out_specs=(big, big, big, any_spec),
        scratch_shapes=[pltpu.SemaphoreType.DMA],
        compiler_params=pltpu.CompilerParams(vmem_limit_bytes=32 << 20),
        name="input_grads",
    )(q, k, v, s, before, after, att)


def on_device(queries, keys, values, out_weight, out_grad):
    grad_scale = 1.0 / math.sqrt(8 * 8192)
    att, scaled, before, after, weight_grad = main_call(
        queries, keys, values, out_weight, out_grad, grad_scale
    )
    query_grad, key_grad, value_grad, attended = grads_call(
        queries, keys, values, scaled, before, after, att
    )
    return attended, query_grad, key_grad, value_grad, weight_grad


def solution(mesh):
    tokens = P("dp", "ctx", None)
    return jax.shard_map(
        on_device,
        mesh=mesh,
        in_specs=(tokens, tokens, tokens, P(), tokens),
        out_specs=(tokens, tokens, tokens, tokens, P(("ctx", "dp"), None)),
        check_vma=False,
    )
```

```python
import functools
import math

import jax
import jax.numpy as jnp
from jax import lax
from jax.experimental import pallas as pl
from jax.experimental.pallas import tpu as pltpu
from jax.sharding import PartitionSpec as P

DK = 128
CH = 256
MESH = pl.DeviceIdType.MESH
BF = jnp.bfloat16
F32 = jnp.float32
PIECES = (
    (0, 256, "yxz"),
    (256, 256, "xzy"),
    (512, 256, "zyx"),
    (768, 256, "yzx"),
    (1024, 256, "xyz"),
    (1280, 256, "zxy"),
    (1536, 256, "yxz"),
    (1792, 128, "xzy"),
    (1920, 128, "zyx"),
)
AXES = "xzy"


def dot_nn(a, b):
    return lax.dot_general(a, b, (((1,), (0,)), ((), ())), preferred_element_type=F32)


def dot_nt(a, b):
    return lax.dot_general(a, b, (((1,), (1,)), ((), ())), preferred_element_type=F32)


def dot_tn(a, b):
    return lax.dot_general(a, b, (((0,), (0,)), ((), ())), preferred_element_type=F32)


def head_cols(h):
    return pl.ds(pl.multiple_of(h * DK, DK), DK)


def masked(product, query_rows):
    rows = lax.broadcasted_iota(jnp.int32, (CH, CH), 0)
    cols = lax.broadcasted_iota(jnp.int32, (CH, CH), 1)
    keep = rows >= cols if query_rows else rows <= cols
    return jnp.where(keep, product, 0.0).astype(BF)


def token_factor(me, shape, axis):
    pos = me * 512 + lax.broadcasted_iota(jnp.int32, shape, axis)
    return lax.rsqrt(((pos + 1) * DK).astype(F32))


def main_kernel(
    grad_scale,
    q_hbm, k_hbm, v_hbm, w_hbm, og_hbm,
    att_hbm, qg_hbm, kg_hbm, vg_hbm, wgrad_hbm,
    qb, kb, vb, wb, ogb, og_mate, scaled, inner_t, att, att_full, att_t, mate_t, weights_t,
    s1, g2, tx_kv, rx_kv, px_kv, before, tx_g, rx_g, px_g, after, wgrad,
    prod, rx1, sum1, rx2, sum2, rx3,
    in_sem, out_sem, og_sem, kv1_s, kv1_r, kv2_s, kv2_r, g1_s, g1_r, g2_s, g2_r,
    mate_s, mate_r, rs_s, rs_r,
):
    me = lax.axis_index("ctx")
    dp = lax.axis_index("dp")
    place = {"x": me // 4, "z": me % 4, "y": dp // 2}
    core = dp % 2
    mate = (me, (dp // 2) * 2 + (1 - core))
    count = 16

    def axis_peer(axis, offset):
        at = dict(place)
        at[axis] = (place[axis] + offset) % 4
        return (at["x"] * 4 + at["z"], at["y"] * 2 + core)

    loads = [
        pltpu.make_async_copy(src.at[0], dst, in_sem.at[n])
        for n, (src, dst) in enumerate(((k_hbm, kb), (v_hbm, vb), (og_hbm, ogb), (q_hbm, qb)))
    ]
    loads.append(pltpu.make_async_copy(w_hbm, wb, in_sem.at[4]))
    loads[0].start()
    loads[1].start()
    loads[2].start()
    loads[4].start()
    loads[3].start()

    barrier = pltpu.get_barrier_semaphore()
    for offset in range(1, count):
        pl.semaphore_signal(
            barrier, inc=1, device_id=((me + offset) % count, dp), device_id_type=MESH
        )
    pl.semaphore_signal(barrier, inc=1, device_id=mate, device_id_type=MESH)
    for offset in range(1, 4):
        pl.semaphore_signal(
            barrier, inc=1, device_id=axis_peer("y", offset), device_id_type=MESH
        )

    loads[0].wait()
    loads[1].wait()

    low, high = slice(0, CH), slice(CH, 2 * CH)

    def kv_one(j, carry):
        wide = pl.ds(pl.multiple_of(j * 256, 256), 256)
        first = dot_tn(vb[low, wide], kb[low, wide])
        both = first + dot_tn(vb[high, wide], kb[high, wide])
        for n in range(2):
            part = slice(n * DK, (n + 1) * DK)
            s1[2 * j + n] = first[part, part].astype(BF)
            tx_kv[2 * j + n] = both[part, part].astype(BF)
        return carry

    lax.fori_loop(0, count // 2, kv_one, 0)
    rx_kv[me] = tx_kv[me]
    pl.semaphore_wait(barrier, count - 1 + 1 + 3)

    def exchange(src, dst, send, recv, offset):
        other = (me + offset) % count
        return pltpu.make_async_remote_copy(
            src_ref=src.at[other], dst_ref=dst.at[me], send_sem=send.at[other],
            recv_sem=recv.at[me], device_id=(other, dp), device_id_type=MESH,
        )

    def arrival(src, dst, send, recv, other):
        return pltpu.make_async_remote_copy(
            src_ref=src.at[other], dst_ref=dst.at[other], send_sem=send.at[other],
            recv_sem=recv.at[other], device_id=(other, dp), device_id_type=MESH,
        )

    def send_all(src, dst, send, recv):
        def one(offset, carry):
            exchange(src, dst, send, recv, offset).start()
            return carry

        lax.fori_loop(1, count, one, 0)

    send_all(tx_kv, rx_kv, kv1_s, kv1_r)

    loads[2].wait()
    og_copy = pltpu.make_async_remote_copy(
        src_ref=ogb, dst_ref=og_mate, send_sem=og_sem.at[0], recv_sem=og_sem.at[1],
        device_id=mate, device_id_type=MESH,
    )
    og_copy.start()

    loads[4].wait()
    loads[3].wait()

    def grad_one(j, carry):
        wide = pl.ds(pl.multiple_of(j * 256, 256), 256)
        grad_out = dot_nt(ogb[...], wb[wide, :]).astype(BF).astype(F32)
        scaled[:, wide] = (grad_out * token_factor(me, (512, 256), 0)).astype(BF)
        late = dot_tn(qb[high, wide], scaled[high, wide])
        both = late + dot_tn(qb[low, wide], scaled[low, wide])
        for n in range(2):
            part = slice(n * DK, (n + 1) * DK)
            g2[2 * j + n] = late[part, part].astype(BF)
            tx_g[2 * j + n] = both[part, part].astype(BF)
        return carry

    lax.fori_loop(0, count // 2, grad_one, 0)
    rx_g[me] = tx_g[me]
    send_all(tx_g, rx_g, g1_s, g1_r)

    def scan(src, dst, send, recv, src2, dst2, send2, recv2, reverse):
        def one(n, total):
            b = count - 1 - n if reverse else n

            @pl.when(b != me)
            def _():
                arrival(src, dst, send, recv, b).wait_recv()

            src2[b] = total.astype(BF)

            @pl.when(b != me)
            def _():
                pltpu.make_async_remote_copy(
                    src_ref=src2.at[b], dst_ref=dst2.at[me], send_sem=send2.at[b],
                    recv_sem=recv2.at[me], device_id=(b, dp), device_id_type=MESH,
                ).start()

            return total + dst[b].astype(F32)

        lax.fori_loop(0, count, one, jnp.zeros((DK, DK), F32))
        dst2[me] = src2[me]

    def finish(src, dst, send, recv, which):
        def one(offset, carry):
            other = (me + offset) % count
            if which == "recv":
                arrival(src, dst, send, recv, other).wait_recv()
            else:
                arrival(src, dst, send, recv, other).wait_send()
            return carry

        lax.fori_loop(1, count, one, 0)

    scan(tx_kv, rx_kv, kv1_s, kv1_r, px_kv, before, kv2_s, kv2_r, False)

    def inner_one(h, carry):
        cols = head_cols(h)
        turned = vb[:, cols].T
        for c, rows in enumerate((low, high)):
            weights_t[h, c] = masked(dot_nt(kb[rows, cols], qb[rows, cols]), False)
            part = dot_nn(turned[:, rows], weights_t[h, c])
            if c == 1:
                part = part + dot_nt(s1[h], qb[rows, cols])
            inner_t[h, :, rows] = part
        return carry

    lax.fori_loop(0, count, inner_one, 0)

    scan(tx_g, rx_g, g1_s, g1_r, px_g, after, g2_s, g2_r, True)

    def mate_copy(h):
        return pltpu.make_async_remote_copy(
            src_ref=att_t.at[1 - core, h], dst_ref=mate_t.at[h], send_sem=mate_s.at[h],
            recv_sem=mate_r.at[h], device_id=mate, device_id_type=MESH,
        )

    def att_one(offset, carry):
        h = (me + offset) % count

        @pl.when(offset > 0)
        def _():
            arrival(px_kv, before, kv2_s, kv2_r, h).wait_recv()

        total = inner_t[h] + dot_nt(before[h], qb[:, head_cols(h)])
        total = (total * token_factor(me, (DK, 512), 1)).astype(BF)
        att_full[h] = total
        for y in range(4):
            for n in range(2):
                first = y * 32 + n * 16
                att_t[n, h, y] = total[first : first + 16]
        mate_copy(h).start()
        return carry

    lax.fori_loop(0, count, att_one, 0)

    og_copy.wait()

    def mate_wait(h, carry):
        mate_copy(h).wait()
        return carry

    lax.fori_loop(0, count, mate_wait, 0)

    def pick(ref, axes, axis, t):
        index = tuple(t if a == axis else slice(None) for a in axes)
        return ref.at[index]

    def rs_copy(p, phase, offset):
        first, width, order = PIECES[p]
        axes = [a for a in AXES if a not in order[:phase]]
        axis = order[phase]
        src = (prod, sum1, sum2)[phase][p]
        dst = (rx1, rx2, rx3)[phase][p]
        return pltpu.make_async_remote_copy(
            src_ref=pick(src, axes, axis, (place[axis] + offset) % 4),
            dst_ref=dst.at[offset - 1],
            send_sem=rs_s.at[phase, p, offset - 1],
            recv_sem=rs_r.at[phase, p, offset - 1],
            device_id=axis_peer(axis, offset), device_id_type=MESH,
        )

    def rs_sum(p, phase):
        first, width, order = PIECES[p]
        axes = [a for a in AXES if a not in order[:phase]]
        axis = order[phase]
        for offset in range(1, 4):
            rs_copy(p, phase, offset).wait_recv()
        src = (prod, sum1, sum2)[phase][p]
        dst = (rx1, rx2, rx3)[phase][p]
        total = pick(src, axes, axis, place[axis])[...].astype(F32)
        for n in range(3):
            total = total + dst[n].astype(F32)
        return total

    for p, (first, width, order) in enumerate(PIECES):
        def prod_half(n, carry, p=p, first=first, width=width):
            rows = pl.ds(n * 8, 8)
            left = att_t[core, rows].reshape(512, 512)
            part = dot_nn(left, ogb[:, first : first + width])
            other = mate_t[rows].reshape(512, 512)
            part = part + dot_nn(other, og_mate[:, first : first + width])
            prod[p][pl.ds(n * 2, 2)] = part.astype(BF).reshape(2, 4, 4, 16, width)
            return carry

        lax.fori_loop(0, 2, prod_half, 0)
        for offset in range(1, 4):
            rs_copy(p, 0, offset).start()

    finish(px_g, after, g2_s, g2_r, "recv")
    results = [att] + [wb.at[pl.ds(n * 512, 512)] for n in range(3)]
    places = (att_hbm, qg_hbm, kg_hbm, vg_hbm)

    def grads_one(h, carry):
        cols = head_cols(h)
        att[:, cols] = att_full[h].T
        before_of = (before[h], (before[h].astype(F32) + s1[h].astype(F32)).astype(BF))
        after_of = ((after[h].astype(F32) + g2[h].astype(F32)).astype(BF), after[h])
        for c, rows in enumerate((low, high)):
            qc, kc, vc, sc = qb[rows, cols], kb[rows, cols], vb[rows, cols], scaled[rows, cols]
            mixing = masked(dot_nt(sc, vc), True)
            mixing_t = masked(dot_nt(vc, sc), False)
            query_grad = dot_nn(mixing, kc) + dot_nn(sc, before_of[c])
            key_grad = dot_nn(mixing_t, qc) + dot_nt(vc, after_of[c])
            value_grad = dot_nn(weights_t[h, c], sc) + dot_nn(kc, after_of[c])
            wb[pl.ds(c * CH, CH), cols] = query_grad.astype(BF)
            wb[pl.ds(512 + c * CH, CH), cols] = key_grad.astype(BF)
            wb[pl.ds(1024 + c * CH, CH), cols] = value_grad.astype(BF)
        return carry

    def results_out(part):
        cols = pl.ds(part * 512, 512)
        return [
            pltpu.make_async_copy(src.at[:, cols], dst.at[:, cols], out_sem.at[n, part])
            for n, (src, dst) in enumerate(zip(results, places))
        ]

    for group in range(4):
        lax.fori_loop(group * 4, group * 4 + 4, grads_one, 0)
        for copy in results_out(group):
            copy.start()
        if group > 0:
            for p in range(3 * group - 3, 3 * group):
                sum1[p][...] = rs_sum(p, 0).astype(BF)
                for offset in range(1, 4):
                    rs_copy(p, 1, offset).start()
    for p in range(len(PIECES)):
        sum2[p][...] = rs_sum(p, 1).astype(BF)
        for offset in range(1, 4):
            rs_copy(p, 2, offset).start()
    for p, (first, width, order) in enumerate(PIECES):
        wgrad[:, first : first + width] = rs_sum(p, 2) * grad_scale
    wgrad_out = pltpu.make_async_copy(wgrad, wgrad_hbm, out_sem.at[4, 0])
    wgrad_out.start()

    finish(tx_kv, rx_kv, kv1_s, kv1_r, "send")
    finish(tx_g, rx_g, g1_s, g1_r, "send")
    finish(px_kv, before, kv2_s, kv2_r, "send")
    finish(px_g, after, g2_s, g2_r, "send")
    for p in range(len(PIECES)):
        for phase in range(3):
            for offset in range(1, 4):
                rs_copy(p, phase, offset).wait_send()
    for group in range(4):
        for copy in results_out(group):
            copy.wait()
    wgrad_out.wait()


def main_call(q, k, v, w, og, grad_scale):
    any_spec = pl.BlockSpec(memory_space=pl.ANY)
    n = len(PIECES)
    widths = [width for _, width, _ in PIECES]
    vm = pltpu.VMEM
    sem = pltpu.SemaphoreType.DMA
    state = vm((16, DK, DK), BF)
    scratch = [
        vm((512, 2048), BF), vm((512, 2048), BF), vm((512, 2048), BF), vm((2048, 2048), BF),
        vm((512, 2048), BF), vm((512, 2048), BF), vm((512, 2048), BF), vm((16, DK, 512), F32),
        vm((512, 2048), BF), vm((16, DK, 512), BF), vm((2, 16, 4, 16, 512), BF),
        vm((16, 4, 16, 512), BF), vm((16, 2, CH, CH), BF),
        state, state, state, state, state, state, state, state, state, state, vm((16, 2048), F32),
        [vm((4, 4, 4, 16, c), BF) for c in widths],
        [vm((3, 4, 4, 16, c), BF) for c in widths],
        [vm((4, 4, 16, c), BF) for c in widths],
        [vm((3, 4, 16, c), BF) for c in widths],
        [vm((4, 16, c), BF) for c in widths],
        [vm((3, 16, c), BF) for c in widths],
        sem((5,)), sem((5, 4)), sem((2,)),
        sem((16,)), sem((16,)), sem((16,)), sem((16,)),
        sem((16,)), sem((16,)), sem((16,)), sem((16,)),
        sem((16,)), sem((16,)), sem((3, n, 3)), sem((3, n, 3)),
    ]
    return pl.pallas_call(
        functools.partial(main_kernel, grad_scale),
        out_shape=(
            jax.ShapeDtypeStruct((512, 2048), BF),
            jax.ShapeDtypeStruct((512, 2048), BF),
            jax.ShapeDtypeStruct((512, 2048), BF),
            jax.ShapeDtypeStruct((512, 2048), BF),
            jax.ShapeDtypeStruct((16, 2048), F32),
        ),
        in_specs=[any_spec] * 5,
        out_specs=(any_spec,) * 5,
        scratch_shapes=scratch,
        compiler_params=pltpu.CompilerParams(
            collective_id=1, has_side_effects=True, vmem_limit_bytes=56 << 20
        ),
        name="states_and_weight_grad",
    )(q, k, v, w, og)


def on_device(queries, keys, values, out_weight, out_grad):
    grad_scale = 1.0 / math.sqrt(8 * 8192)
    *inner, weight_grad = main_call(queries, keys, values, out_weight, out_grad, grad_scale)
    return (*(x[None] for x in inner), weight_grad)


def solution(mesh):
    tokens = P("dp", "ctx", None)
    return jax.shard_map(
        on_device,
        mesh=mesh,
        in_specs=(tokens, tokens, tokens, P(), tokens),
        out_specs=(tokens, tokens, tokens, tokens, P(("ctx", "dp"), None)),
        check_vma=False,
    )
```

```python
import functools
import math

import jax
import jax.numpy as jnp
from jax import lax
from jax.experimental import pallas as pl
from jax.experimental.pallas import tpu as pltpu
from jax.sharding import PartitionSpec as P

DK = 128
CH = 256
MESH = pl.DeviceIdType.MESH
BF = jnp.bfloat16
F32 = jnp.float32
PIECES = (
    (0, 256, "yxz"),
    (256, 256, "xzy"),
    (512, 256, "zyx"),
    (768, 256, "yzx"),
    (1024, 256, "xyz"),
    (1280, 256, "zxy"),
    (1536, 256, "yxz"),
    (1792, 128, "xzy"),
    (1920, 128, "zyx"),
)
AXES = "xzy"


def dot_nn(a, b):
    return lax.dot_general(a, b, (((1,), (0,)), ((), ())), preferred_element_type=F32)


def dot_nt(a, b):
    return lax.dot_general(a, b, (((1,), (1,)), ((), ())), preferred_element_type=F32)


def dot_tn(a, b):
    return lax.dot_general(a, b, (((0,), (0,)), ((), ())), preferred_element_type=F32)


def head_cols(h):
    return pl.ds(pl.multiple_of(h * DK, DK), DK)


def masked(product, query_rows):
    rows = lax.broadcasted_iota(jnp.int32, (CH, CH), 0)
    cols = lax.broadcasted_iota(jnp.int32, (CH, CH), 1)
    keep = rows >= cols if query_rows else rows <= cols
    return jnp.where(keep, product, 0.0).astype(BF)


def token_factor(me, shape, axis):
    pos = me * 512 + lax.broadcasted_iota(jnp.int32, shape, axis)
    return lax.rsqrt(((pos + 1) * DK).astype(F32))


def main_kernel(
    grad_scale,
    q_hbm, k_hbm, v_hbm, w_hbm, og_hbm,
    att, qg, kg, vg, wgrad,
    qb, kb, vb, wb, og_both, scaled, inner_t, att_full, at_both, weights_t,
    s1, g2, tx_kv, rx_kv, px_kv, before, tx_g, rx_g, px_g, after,
    prod, rx1, sum1, rx2, sum2, rx3,
    in_sem, og_sem, kv1_s, kv1_r, kv2_s, kv2_r, g1_s, g1_r, g2_s, g2_r,
    mate_s, mate_r, rs_s, rs_r,
):
    me = lax.axis_index("ctx")
    dp = lax.axis_index("dp")
    place = {"x": me // 4, "z": me % 4, "y": dp // 2}
    core = dp % 2
    mate = (me, (dp // 2) * 2 + (1 - core))
    count = 16

    def axis_peer(axis, offset):
        at = dict(place)
        at[axis] = (place[axis] + offset) % 4
        return (at["x"] * 4 + at["z"], at["y"] * 2 + core)

    def by_head(first, last, one):
        def several(n, carry):
            for m in range(2):
                one(first + 2 * n + m, carry)
            return carry

        lax.fori_loop(0, (last - first) // 2, several, 0)

    loads = [
        pltpu.make_async_copy(src.at[0], dst, in_sem.at[n])
        for n, (src, dst) in enumerate(((k_hbm, kb), (v_hbm, vb), (og_hbm, og_both.at[0:512]), (q_hbm, qb)))
    ]
    loads.append(pltpu.make_async_copy(w_hbm, wb, in_sem.at[4]))
    loads[0].start()
    loads[1].start()

    barrier = pltpu.get_barrier_semaphore()
    for offset in range(1, count):
        pl.semaphore_signal(
            barrier, inc=1, device_id=((me + offset) % count, dp), device_id_type=MESH
        )
    pl.semaphore_signal(barrier, inc=1, device_id=mate, device_id_type=MESH)
    for offset in range(1, 4):
        pl.semaphore_signal(
            barrier, inc=1, device_id=axis_peer("y", offset), device_id_type=MESH
        )

    loads[0].wait()
    loads[1].wait()
    loads[2].start()
    loads[4].start()
    loads[3].start()
    low, high = slice(0, CH), slice(CH, 2 * CH)

    def pair_at(j):
        return (me // 2 + 1 + j) % (count // 2)

    def kv_one(j, carry):
        j = pair_at(j)
        wide = pl.ds(pl.multiple_of(j * 256, 256), 256)
        first = dot_tn(vb[low, wide], kb[low, wide])
        both = first + dot_tn(vb[high, wide], kb[high, wide])
        for n in range(2):
            part = slice(n * DK, (n + 1) * DK)
            s1[2 * j + n] = first[part, part].astype(BF)
            tx_kv[2 * j + n] = both[part, part].astype(BF)
        return carry

    def arrival(src, dst, send, recv, other):
        return pltpu.make_async_remote_copy(
            src_ref=src.at[other], dst_ref=dst.at[other], send_sem=send.at[other],
            recv_sem=recv.at[other], device_id=(other, dp), device_id_type=MESH,
        )

    def send_one(src, dst, send, recv, other):
        @pl.when(other != me)
        def _():
            pltpu.make_async_remote_copy(
                src_ref=src.at[other], dst_ref=dst.at[me], send_sem=send.at[other],
                recv_sem=recv.at[me], device_id=(other, dp), device_id_type=MESH,
            ).start()

    def send_all(src, dst, send, recv):
        def one(n, carry):
            send_one(src, dst, send, recv, (me + n) % count)
            return carry

        lax.fori_loop(1, count, one, 0)

    def kv_send(j, carry):
        kv_one(j, carry)
        for n in range(2):
            send_one(tx_kv, rx_kv, kv1_s, kv1_r, 2 * pair_at(j) + n)
        return carry

    def kv_sent(j, carry):
        for n in range(2):
            send_one(tx_kv, rx_kv, kv1_s, kv1_r, 2 * pair_at(j) + n)
        return carry

    lax.fori_loop(0, count // 4, kv_one, 0)
    pl.semaphore_wait(barrier, count - 1 + 1 + 3)
    lax.fori_loop(0, count // 4, kv_sent, 0)
    lax.fori_loop(count // 4, count // 2, kv_send, 0)
    rx_kv[me] = tx_kv[me]

    loads[2].wait()
    og_copy = pltpu.make_async_remote_copy(
        src_ref=og_both.at[0:512], dst_ref=og_both.at[512:1024], send_sem=og_sem.at[0], recv_sem=og_sem.at[1],
        device_id=mate, device_id_type=MESH,
    )
    og_copy.start()

    loads[4].wait()
    loads[3].wait()

    def grad_out_of(j):
        wide = pl.ds(pl.multiple_of(pair_at(j) * 256, 256), 256)
        grad_out = dot_nt(og_both[0:512], wb[wide, :]).astype(BF).astype(F32)
        scaled[:, wide] = (grad_out * token_factor(me, (512, 256), 0)).astype(BF)

    def grad_state_of(j):
        j = pair_at(j)
        wide = pl.ds(pl.multiple_of(j * 256, 256), 256)
        late = dot_tn(qb[high, wide], scaled[high, wide])
        both = late + dot_tn(qb[low, wide], scaled[low, wide])
        for n in range(2):
            part = slice(n * DK, (n + 1) * DK)
            g2[2 * j + n] = late[part, part].astype(BF)
            tx_g[2 * j + n] = both[part, part].astype(BF)
            send_one(tx_g, rx_g, g1_s, g1_r, 2 * j + n)

    def grad_one(j, carry):
        grad_state_of(j - 1)
        grad_out_of(j)
        return carry

    grad_out_of(0)
    lax.fori_loop(1, count // 2, grad_one, 0)
    grad_state_of(count // 2 - 1)
    rx_g[me] = tx_g[me]

    def scan(src, dst, send, recv, src2, dst2, send2, recv2, reverse):
        def one(n, total):
            b = count - 1 - n if reverse else n

            @pl.when(b != me)
            def _():
                arrival(src, dst, send, recv, b).wait_recv()

            src2[b] = total.astype(BF)

            return total + dst[b].astype(F32)

        lax.fori_loop(0, count, one, jnp.zeros((DK, DK), F32))
        dst2[me] = src2[me]
        send_all(src2, dst2, send2, recv2)

    def finish(src, dst, send, recv, which):
        def one(offset, carry):
            other = (me + offset) % count
            if which == "recv":
                arrival(src, dst, send, recv, other).wait_recv()
            else:
                arrival(src, dst, send, recv, other).wait_send()
            return carry

        lax.fori_loop(1, count, one, 0)

    scan(tx_kv, rx_kv, kv1_s, kv1_r, px_kv, before, kv2_s, kv2_r, False)

    def inner_one(h, carry):
        cols = head_cols(h)
        turned = vb[:, cols].T
        for c, rows in enumerate((low, high)):
            weights_t[h, c] = masked(dot_nt(kb[rows, cols], qb[rows, cols]), False)
            part = dot_nn(turned[:, rows], weights_t[h, c])
            if c == 1:
                part = part + dot_nt(s1[h], qb[rows, cols])
            inner_t[h, :, rows] = part
        return carry

    by_head(0, count, inner_one)
    scan(tx_g, rx_g, g1_s, g1_r, px_g, after, g2_s, g2_r, True)

    def mate_copy(h):
        return pltpu.make_async_remote_copy(
            src_ref=att_full.at[h, :, 1 - core], dst_ref=at_both.at[h, :, :, pl.ds(512, 512)], send_sem=mate_s.at[h],
            recv_sem=mate_r.at[h], device_id=mate, device_id_type=MESH,
        )

    def att_one(offset, carry):
        h = (me + count - offset) % count

        @pl.when(offset > 0)
        def _():
            arrival(px_kv, before, kv2_s, kv2_r, h).wait_recv()

        total = inner_t[h] + dot_nt(before[h], qb[:, head_cols(h)])
        total = (total * token_factor(me, (DK, 512), 1)).astype(BF)
        att_full[h] = total.reshape(4, 2, 16, 512)
        at_both[h, :, :, 0:512] = att_full[h, :, core]
        mate_copy(h).start()
        return carry

    lax.fori_loop(0, count, att_one, 0)

    og_copy.wait()

    def mate_wait(h, carry):
        mate_copy(h).wait()
        return carry

    lax.fori_loop(0, count, mate_wait, 0)

    def pick(ref, axes, axis, t):
        index = tuple(t if a == axis else slice(None) for a in axes)
        return ref.at[index]

    def rs_copy(p, phase, offset):
        first, width, order = PIECES[p]
        axes = [a for a in AXES if a not in order[:phase]]
        axis = order[phase]
        src = (prod, sum1, sum2)[phase][p]
        dst = (rx1, rx2, rx3)[phase][p]
        return pltpu.make_async_remote_copy(
            src_ref=pick(src, axes, axis, (place[axis] + offset) % 4),
            dst_ref=dst.at[offset - 1],
            send_sem=rs_s.at[phase, p, offset - 1],
            recv_sem=rs_r.at[phase, p, offset - 1],
            device_id=axis_peer(axis, offset), device_id_type=MESH,
        )

    def rs_sum(p, phase):
        first, width, order = PIECES[p]
        axes = [a for a in AXES if a not in order[:phase]]
        axis = order[phase]
        for offset in range(1, 4):
            rs_copy(p, phase, offset).wait_recv()
        src = (prod, sum1, sum2)[phase][p]
        dst = (rx1, rx2, rx3)[phase][p]
        total = pick(src, axes, axis, place[axis])[...].astype(F32)
        for n in range(3):
            total = total + dst[n].astype(F32)
        return total

    for p, (first, width, order) in enumerate(PIECES):
        left = at_both[...].reshape(1024, 1024)
        part = dot_nn(left, og_both[:, first : first + width])
        prod[p][...] = part.astype(BF).reshape(4, 4, 4, 16, width)
        if p < 3:
            for offset in range(1, 4):
                rs_copy(p, 0, offset).start()

    def query_one(h, carry):
        cols = head_cols(h)
        att[:, cols] = att_full[h].reshape(DK, 512).T
        before_of = (before[h], (before[h].astype(F32) + s1[h].astype(F32)).astype(BF))
        for c, rows in enumerate((low, high)):
            kc, vc, sc = kb[rows, cols], vb[rows, cols], scaled[rows, cols]
            mixing = masked(dot_nt(sc, vc), True)
            query_grad = dot_nn(mixing, kc) + dot_nn(sc, before_of[c])
            qg[rows, cols] = query_grad.astype(BF)
        return carry

    def key_one(h, carry):
        cols = head_cols(h)
        after_of = ((after[h].astype(F32) + g2[h].astype(F32)).astype(BF), after[h])
        for c, rows in enumerate((low, high)):
            qc, kc, vc, sc = qb[rows, cols], kb[rows, cols], vb[rows, cols], scaled[rows, cols]
            mixing_t = masked(dot_nt(vc, sc), False)
            key_grad = dot_nn(mixing_t, qc) + dot_nt(vc, after_of[c])
            value_grad = dot_nn(weights_t[h, c], sc) + dot_nn(kc, after_of[c])
            kg[rows, cols] = key_grad.astype(BF)
            vg[rows, cols] = value_grad.astype(BF)
        return carry

    def second_phase(pieces):
        for p in pieces:
            sum1[p][...] = rs_sum(p, 0).astype(BF)
            for offset in range(1, 4):
                rs_copy(p, 1, offset).start()

    def third_phase(pieces):
        for p in pieces:
            sum2[p][...] = rs_sum(p, 1).astype(BF)
            for offset in range(1, 4):
                rs_copy(p, 2, offset).start()

    def first_phase(pieces):
        for p in pieces:
            for offset in range(1, 4):
                rs_copy(p, 0, offset).start()

    first_phase(range(3, 6))
    by_head(0, count, query_one)
    second_phase(range(0, 3))
    first_phase(range(6, 9))
    finish(px_g, after, g2_s, g2_r, "recv")
    by_head(0, 8, key_one)
    second_phase(range(3, 6))
    by_head(8, count, key_one)
    third_phase(range(0, 3))
    second_phase(range(6, 9))
    third_phase(range(3, 9))
    for p, (first, width, order) in enumerate(PIECES):
        wgrad[:, first : first + width] = rs_sum(p, 2) * grad_scale
    finish(tx_kv, rx_kv, kv1_s, kv1_r, "send")
    finish(tx_g, rx_g, g1_s, g1_r, "send")
    finish(px_kv, before, kv2_s, kv2_r, "send")
    finish(px_g, after, g2_s, g2_r, "send")
    for p in range(len(PIECES)):
        for phase in range(3):
            for offset in range(1, 4):
                rs_copy(p, phase, offset).wait_send()

def main_call(q, k, v, w, og, grad_scale):
    any_spec = pl.BlockSpec(memory_space=pl.ANY)
    n = len(PIECES)
    widths = [width for _, width, _ in PIECES]
    vm = pltpu.VMEM
    sem = pltpu.SemaphoreType.DMA
    state = vm((16, DK, DK), BF)
    scratch = [
        vm((512, 2048), BF), vm((512, 2048), BF), vm((512, 2048), BF), vm((2048, 2048), BF),
        vm((1024, 2048), BF), vm((512, 2048), BF), vm((16, DK, 512), F32),
        vm((16, 4, 2, 16, 512), BF), vm((16, 4, 16, 1024), BF), vm((16, 2, CH, CH), BF),
        state, state, state, state, state, state, state, state, state, state,
        [vm((4, 4, 4, 16, c), BF) for c in widths],
        [vm((3, 4, 4, 16, c), BF) for c in widths],
        [vm((4, 4, 16, c), BF) for c in widths],
        [vm((3, 4, 16, c), BF) for c in widths],
        [vm((4, 16, c), BF) for c in widths],
        [vm((3, 16, c), BF) for c in widths],
        sem((5,)), sem((2,)),
        sem((16,)), sem((16,)), sem((16,)), sem((16,)),
        sem((16,)), sem((16,)), sem((16,)), sem((16,)),
        sem((16,)), sem((16,)), sem((3, n, 3)), sem((3, n, 3)),
    ]
    return pl.pallas_call(
        functools.partial(main_kernel, grad_scale),
        out_shape=(vm((512, 2048), BF),) * 4 + (vm((16, 2048), F32),),
        in_specs=[any_spec] * 5,
        out_specs=(pl.BlockSpec(memory_space=vm),) * 5,
        scratch_shapes=scratch,
        compiler_params=pltpu.CompilerParams(
            collective_id=1, has_side_effects=True, vmem_limit_bytes=50 << 20
        ),
        name="states_and_weight_grad",
    )(q, k, v, w, og)


def place_kernel(*refs):
    sem = refs[-1]
    copies = []
    for n in range(4):
        for half in range(2):
            rows = pl.ds(half * 256, 256)
            copies.append(
                pltpu.make_async_copy(
                    refs[n].at[rows], refs[5 + n].at[0, rows], sem.at[2 * n + half]
                )
            )
    copies.append(pltpu.make_async_copy(refs[4], refs[9], sem.at[8]))
    for copy in copies:
        copy.start()
    for copy in copies:
        copy.wait()


def place_call(*arrays):
    any_spec = pl.BlockSpec(memory_space=pl.ANY)
    return pl.pallas_call(
        place_kernel,
        out_shape=(jax.ShapeDtypeStruct((1, 512, 2048), BF),) * 4
        + (jax.ShapeDtypeStruct((16, 2048), F32),),
        in_specs=[pl.BlockSpec(memory_space=pltpu.VMEM)] * 5,
        out_specs=(any_spec,) * 5,
        scratch_shapes=[pltpu.SemaphoreType.DMA((9,))],
        compiler_params=pltpu.CompilerParams(vmem_limit_bytes=2 << 20),
        name="place_outputs",
    )(*arrays)


def on_device(queries, keys, values, out_weight, out_grad):
    grad_scale = 1.0 / math.sqrt(8 * 8192)
    inner = main_call(queries, keys, values, out_weight, out_grad, grad_scale)
    return place_call(*(pltpu.with_memory_space_constraint(x, pltpu.VMEM) for x in inner))


def solution(mesh):
    tokens = P("dp", "ctx", None)
    return jax.shard_map(
        on_device,
        mesh=mesh,
        in_specs=(tokens, tokens, tokens, P(), tokens),
        out_specs=(tokens, tokens, tokens, tokens, P(("ctx", "dp"), None)),
        check_vma=False,
    )
```

```python
import functools
import math

import jax
import jax.numpy as jnp
from jax import lax
from jax.experimental import pallas as pl
from jax.experimental.pallas import tpu as pltpu
from jax.sharding import PartitionSpec as P

DK = 128
CH = 256
MESH = pl.DeviceIdType.MESH
BF = jnp.bfloat16
F32 = jnp.float32
PIECES = (
    (0, 384, "yxz", 0),
    (384, 384, "yzx", 1),
    (768, 384, "zxy", 0),
    (1152, 384, "zyx", 1),
    (1536, 256, "xyz", 0),
    (1792, 256, "xzy", 1),
)
AXES = "xzy"


def dot_nn(a, b):
    return lax.dot_general(a, b, (((1,), (0,)), ((), ())), preferred_element_type=F32)


def dot_nt(a, b):
    return lax.dot_general(a, b, (((1,), (1,)), ((), ())), preferred_element_type=F32)


def dot_tn(a, b):
    return lax.dot_general(a, b, (((0,), (0,)), ((), ())), preferred_element_type=F32)


def head_cols(h):
    return pl.ds(pl.multiple_of(h * DK, DK), DK)


def masked(product, query_rows):
    rows = lax.broadcasted_iota(jnp.int32, (CH, CH), 0)
    cols = lax.broadcasted_iota(jnp.int32, (CH, CH), 1)
    keep = rows >= cols if query_rows else rows <= cols
    return jnp.where(keep, product, 0.0).astype(BF)


def token_factor(me, shape, axis):
    pos = me * 512 + lax.broadcasted_iota(jnp.int32, shape, axis)
    return lax.rsqrt(((pos + 1) * DK).astype(F32))


def main_kernel(
    grad_scale,
    q_hbm, k_hbm, v_hbm, w_hbm, og_hbm,
    att, qg, kg, vg, wgrad,
    qb, kb, vb, wb, og_both, scaled, inner_t, att_full, at_both, weights_t,
    s1, g2, tx_kv, rx_kv, px_kv, before, tx_g, rx_g, px_g, after,
    prod, rx1, sum1, rx2, sum2, rx3, middle,
    in_sem, og_sem, kv1_s, kv1_r, kv2_s, kv2_r, g1_s, g1_r, g2_s, g2_r,
    mate_s, mate_r, rs_s, rs_r,
):
    me = lax.axis_index("ctx")
    dp = lax.axis_index("dp")
    place = {"x": me // 4, "z": me % 4, "y": dp // 2}
    core = dp % 2
    mate = (me, (dp // 2) * 2 + (1 - core))
    count = 16

    def axis_peer(axis, to):
        at = dict(place)
        at[axis] = to
        return (at["x"] * 4 + at["z"], at["y"] * 2 + core)

    def by_head(first, last, one):
        def several(n, carry):
            for m in range(2):
                one(first + 2 * n + m, carry)
            return carry

        lax.fori_loop(0, (last - first) // 2, several, 0)

    loads = [
        pltpu.make_async_copy(src.at[0], dst, in_sem.at[n])
        for n, (src, dst) in enumerate(((k_hbm, kb), (v_hbm, vb), (og_hbm, og_both.at[0:512]), (q_hbm, qb)))
    ]
    loads.append(pltpu.make_async_copy(w_hbm, wb, in_sem.at[4]))
    loads[0].start()
    loads[1].start()

    barrier = pltpu.get_barrier_semaphore()
    for offset in range(1, count):
        pl.semaphore_signal(
            barrier, inc=1, device_id=((me + offset) % count, dp), device_id_type=MESH
        )
    pl.semaphore_signal(barrier, inc=1, device_id=mate, device_id_type=MESH)
    for offset in (1, 3):
        pl.semaphore_signal(
            barrier, inc=1, device_id=axis_peer("y", (place["y"] + offset) % 4), device_id_type=MESH
        )

    loads[0].wait()
    loads[1].wait()
    loads[2].start()
    loads[4].start()
    loads[3].start()
    low, high = slice(0, CH), slice(CH, 2 * CH)

    def pair_at(j):
        return (me // 2 + 1 + j) % (count // 2)

    def kv_one(j, carry):
        j = pair_at(j)
        wide = pl.ds(pl.multiple_of(j * 256, 256), 256)
        first = dot_tn(vb[low, wide], kb[low, wide])
        both = first + dot_tn(vb[high, wide], kb[high, wide])
        for n in range(2):
            part = slice(n * DK, (n + 1) * DK)
            s1[2 * j + n] = first[part, part].astype(BF)
            tx_kv[2 * j + n] = both[part, part].astype(BF)
        return carry

    def arrival(src, dst, send, recv, other):
        return pltpu.make_async_remote_copy(
            src_ref=src.at[other], dst_ref=dst.at[other], send_sem=send.at[other],
            recv_sem=recv.at[other], device_id=(other, dp), device_id_type=MESH,
        )

    def send_one(src, dst, send, recv, other):
        @pl.when(other != me)
        def _():
            pltpu.make_async_remote_copy(
                src_ref=src.at[other], dst_ref=dst.at[me], send_sem=send.at[other],
                recv_sem=recv.at[me], device_id=(other, dp), device_id_type=MESH,
            ).start()

    def send_all(src, dst, send, recv):
        def one(n, carry):
            send_one(src, dst, send, recv, (me + n) % count)
            return carry

        lax.fori_loop(1, count, one, 0)

    def kv_send(j, carry):
        kv_one(j, carry)
        for n in range(2):
            send_one(tx_kv, rx_kv, kv1_s, kv1_r, 2 * pair_at(j) + n)
        return carry

    def kv_sent(j, carry):
        for n in range(2):
            send_one(tx_kv, rx_kv, kv1_s, kv1_r, 2 * pair_at(j) + n)
        return carry

    lax.fori_loop(0, count // 4, kv_one, 0)
    pl.semaphore_wait(barrier, count - 1 + 1 + 2)
    lax.fori_loop(0, count // 4, kv_sent, 0)
    lax.fori_loop(count // 4, count // 2, kv_send, 0)
    rx_kv[me] = tx_kv[me]

    loads[2].wait()
    og_copy = pltpu.make_async_remote_copy(
        src_ref=og_both.at[0:512], dst_ref=og_both.at[512:1024], send_sem=og_sem.at[0], recv_sem=og_sem.at[1],
        device_id=mate, device_id_type=MESH,
    )
    og_copy.start()

    def scan(src, dst, send, recv, src2, dst2, send2, recv2, reverse):
        def one(n, total):
            b = count - 1 - n if reverse else n

            @pl.when(b != me)
            def _():
                arrival(src, dst, send, recv, b).wait_recv()

            src2[b] = total.astype(BF)

            return total + dst[b].astype(F32)

        lax.fori_loop(0, count, one, jnp.zeros((DK, DK), F32))
        dst2[me] = src2[me]
        send_all(src2, dst2, send2, recv2)

    def finish(src, dst, send, recv, which):
        def one(offset, carry):
            other = (me + offset) % count
            if which == "recv":
                arrival(src, dst, send, recv, other).wait_recv()
            else:
                arrival(src, dst, send, recv, other).wait_send()
            return carry

        lax.fori_loop(1, count, one, 0)

    loads[4].wait()
    loads[3].wait()

    def grad_out_of(j):
        wide = pl.ds(pl.multiple_of(pair_at(j) * 256, 256), 256)
        grad_out = dot_nt(og_both[0:512], wb[wide, :]).astype(BF).astype(F32)
        scaled[:, wide] = (grad_out * token_factor(me, (512, 256), 0)).astype(BF)

    def grad_state_of(j):
        j = pair_at(j)
        wide = pl.ds(pl.multiple_of(j * 256, 256), 256)
        late = dot_tn(qb[high, wide], scaled[high, wide])
        both = late + dot_tn(qb[low, wide], scaled[low, wide])
        for n in range(2):
            part = slice(n * DK, (n + 1) * DK)
            g2[2 * j + n] = late[part, part].astype(BF)
            tx_g[2 * j + n] = both[part, part].astype(BF)

    def grad_one(j, carry):
        grad_state_of(j - 1)
        grad_out_of(j)
        return carry

    grad_out_of(0)
    lax.fori_loop(1, 6, grad_one, 0)
    scan(tx_kv, rx_kv, kv1_s, kv1_r, px_kv, before, kv2_s, kv2_r, False)
    lax.fori_loop(6, count // 2, grad_one, 0)
    grad_state_of(count // 2 - 1)
    rx_g[me] = tx_g[me]
    send_all(tx_g, rx_g, g1_s, g1_r)


    def inner_one(h, carry):
        cols = head_cols(h)
        turned = vb[:, cols].T
        for c, rows in enumerate((low, high)):
            weights_t[h, c] = masked(dot_nt(kb[rows, cols], qb[rows, cols]), False)
            part = dot_nn(turned[:, rows], weights_t[h, c])
            if c == 1:
                part = part + dot_nt(s1[h], qb[rows, cols])
            inner_t[h, :, rows] = part
        return carry

    by_head(0, count, inner_one)

    def mate_copy(h):
        return pltpu.make_async_remote_copy(
            src_ref=att_full.at[h, :, 1 - core], dst_ref=at_both.at[h, :, :, pl.ds(512, 512)], send_sem=mate_s.at[h],
            recv_sem=mate_r.at[h], device_id=mate, device_id_type=MESH,
        )

    def att_one(offset, carry):
        h = (me + count - offset) % count

        @pl.when(offset > 0)
        def _():
            arrival(px_kv, before, kv2_s, kv2_r, h).wait_recv()

        total = inner_t[h] + dot_nt(before[h], qb[:, head_cols(h)])
        total = (total * token_factor(me, (DK, 512), 1)).astype(BF)
        att_full[h] = total.reshape(4, 2, 16, 512)
        at_both[h, :, :, 0:512] = att_full[h, :, core]
        mate_copy(h).start()
        return carry

    lax.fori_loop(0, count, att_one, 0)
    scan(tx_g, rx_g, g1_s, g1_r, px_g, after, g2_s, g2_r, True)

    og_copy.wait()

    def mate_wait(h, carry):
        mate_copy(h).wait()
        return carry

    lax.fori_loop(0, count, mate_wait, 0)

    def pick(ref, axes, axis, t):
        index = tuple(t if a == axis else slice(None) for a in axes)
        return ref.at[index]

    def partners(p, c):
        pair = (c + 1 - 2 * (c % 2), 3 - c)
        return pair if PIECES[p][3] == 0 else pair[::-1]

    def rs_parts(p, phase):
        order = PIECES[p][2]
        axes = [a for a in AXES if a not in order[:phase]]
        axis = order[phase]
        return (prod, sum1, sum2)[phase][p], (rx1, rx2, rx3)[phase][p], axes, axis

    def rs_copy(p, phase, slot):
        src, dst, axes, axis = rs_parts(p, phase)
        one, two = partners(p, place[axis])
        if phase > 0:
            to = (place[axis] + slot + 1) % 4
            out = pick(src, axes, axis, to)
        elif slot == 0:
            out, to = pick(src, axes, axis, one), one
        elif slot == 1:
            out, to = pick(src, axes, axis, partners(p, one)[1]), one
        else:
            out, to = middle[p], two
        return pltpu.make_async_remote_copy(
            src_ref=out, dst_ref=dst.at[slot],
            send_sem=rs_s.at[phase, p, slot], recv_sem=rs_r.at[phase, p, slot],
            device_id=axis_peer(axis, to), device_id_type=MESH,
        )

    def rs_begin(p, phase):
        for slot in (1, 0) if phase == 0 else (0, 2, 1):
            rs_copy(p, phase, slot).start()

    def rs_mid(p):
        src, dst, axes, axis = rs_parts(p, 0)
        two = partners(p, place[axis])[1]
        rs_copy(p, 0, 1).wait_recv()
        total = pick(src, axes, axis, two)[...].astype(F32) + dst[1].astype(F32)
        middle[p][...] = total.astype(BF)
        rs_copy(p, 0, 2).start()

    def rs_sum(p, phase):
        src, dst, axes, axis = rs_parts(p, phase)
        slots = (0, 2) if phase == 0 else (0, 1, 2)
        for slot in slots:
            rs_copy(p, phase, slot).wait_recv()
        total = pick(src, axes, axis, place[axis])[...].astype(F32)
        for slot in slots:
            total = total + dst[slot].astype(F32)
        return total

    for p, (first, width, _, _) in enumerate(PIECES):
        left = at_both[...].reshape(1024, 1024)
        part = dot_nn(left, og_both[:, first : first + width])
        prod[p][...] = part.astype(BF).reshape(4, 4, 4, 16, width)
        rs_begin(p, 0)

    def query_one(h, carry):
        cols = head_cols(h)
        att[:, cols] = att_full[h].reshape(DK, 512).T
        before_of = (before[h], (before[h].astype(F32) + s1[h].astype(F32)).astype(BF))
        for c, rows in enumerate((low, high)):
            kc, vc, sc = kb[rows, cols], vb[rows, cols], scaled[rows, cols]
            mixing = masked(dot_nt(sc, vc), True)
            query_grad = dot_nn(mixing, kc) + dot_nn(sc, before_of[c])
            qg[rows, cols] = query_grad.astype(BF)
        return carry

    def key_one(h, carry):
        cols = head_cols(h)
        after_of = ((after[h].astype(F32) + g2[h].astype(F32)).astype(BF), after[h])
        for c, rows in enumerate((low, high)):
            qc, kc, vc, sc = qb[rows, cols], kb[rows, cols], vb[rows, cols], scaled[rows, cols]
            mixing_t = masked(dot_nt(vc, sc), False)
            key_grad = dot_nn(mixing_t, qc) + dot_nt(vc, after_of[c])
            value_grad = dot_nn(weights_t[h, c], sc) + dot_nn(kc, after_of[c])
            kg[rows, cols] = key_grad.astype(BF)
            vg[rows, cols] = value_grad.astype(BF)
        return carry

    def next_phase(phase):
        for p in range(len(PIECES)):
            (sum1, sum2)[phase - 1][p][...] = rs_sum(p, phase - 1).astype(BF)
            rs_begin(p, phase)

    by_head(0, count, query_one)
    for p in range(len(PIECES)):
        rs_mid(p)
    next_phase(1)
    finish(px_g, after, g2_s, g2_r, "recv")
    by_head(0, 10, key_one)
    next_phase(2)
    by_head(10, 16, key_one)
    for p, (first, width, _, _) in enumerate(PIECES):
        wgrad[:, first : first + width] = rs_sum(p, 2) * grad_scale
    finish(tx_kv, rx_kv, kv1_s, kv1_r, "send")
    finish(tx_g, rx_g, g1_s, g1_r, "send")
    finish(px_kv, before, kv2_s, kv2_r, "send")
    finish(px_g, after, g2_s, g2_r, "send")
    for p in range(len(PIECES)):
        for phase in range(3):
            for slot in range(3):
                rs_copy(p, phase, slot).wait_send()

def main_call(q, k, v, w, og, grad_scale):
    any_spec = pl.BlockSpec(memory_space=pl.ANY)
    n = len(PIECES)
    widths = [width for _, width, _, _ in PIECES]
    vm = pltpu.VMEM
    sem = pltpu.SemaphoreType.DMA
    state = vm((16, DK, DK), BF)
    scratch = [
        vm((512, 2048), BF), vm((512, 2048), BF), vm((512, 2048), BF), vm((2048, 2048), BF),
        vm((1024, 2048), BF), vm((512, 2048), BF), vm((16, DK, 512), F32),
        vm((16, 4, 2, 16, 512), BF), vm((16, 4, 16, 1024), BF), vm((16, 2, CH, CH), BF),
        state, state, state, state, state, state, state, state, state, state,
        [vm((4, 4, 4, 16, c), BF) for c in widths],
        [vm((3, 4, 4, 16, c), BF) for c in widths],
        [vm((4, 4, 16, c), BF) for c in widths],
        [vm((3, 4, 16, c), BF) for c in widths],
        [vm((4, 16, c), BF) for c in widths],
        [vm((3, 16, c), BF) for c in widths],
        [vm((4, 4, 16, c), BF) for c in widths],
        sem((5,)), sem((2,)),
        sem((16,)), sem((16,)), sem((16,)), sem((16,)),
        sem((16,)), sem((16,)), sem((16,)), sem((16,)),
        sem((16,)), sem((16,)), sem((3, n, 3)), sem((3, n, 3)),
    ]
    return pl.pallas_call(
        functools.partial(main_kernel, grad_scale),
        out_shape=(vm((512, 2048), BF),) * 4 + (vm((16, 2048), F32),),
        in_specs=[any_spec] * 5,
        out_specs=(pl.BlockSpec(memory_space=vm),) * 5,
        scratch_shapes=scratch,
        compiler_params=pltpu.CompilerParams(
            collective_id=1, has_side_effects=True, vmem_limit_bytes=52 << 20
        ),
        name="states_and_weight_grad",
    )(q, k, v, w, og)


def place_kernel(*refs):
    sem = refs[-1]
    copies = []
    for n in range(4):
        for half in range(2):
            rows = pl.ds(half * 256, 256)
            copies.append(
                pltpu.make_async_copy(
                    refs[n].at[rows], refs[5 + n].at[0, rows], sem.at[2 * n + half]
                )
            )
    copies.append(pltpu.make_async_copy(refs[4], refs[9], sem.at[8]))
    for copy in copies:
        copy.start()
    for copy in copies:
        copy.wait()


def place_call(*arrays):
    any_spec = pl.BlockSpec(memory_space=pl.ANY)
    return pl.pallas_call(
        place_kernel,
        out_shape=(jax.ShapeDtypeStruct((1, 512, 2048), BF),) * 4
        + (jax.ShapeDtypeStruct((16, 2048), F32),),
        in_specs=[pl.BlockSpec(memory_space=pltpu.VMEM)] * 5,
        out_specs=(any_spec,) * 5,
        scratch_shapes=[pltpu.SemaphoreType.DMA((9,))],
        compiler_params=pltpu.CompilerParams(vmem_limit_bytes=2 << 20),
        name="place_outputs",
    )(*arrays)


def on_device(queries, keys, values, out_weight, out_grad):
    grad_scale = 1.0 / math.sqrt(8 * 8192)
    inner = main_call(queries, keys, values, out_weight, out_grad, grad_scale)
    return place_call(*(pltpu.with_memory_space_constraint(x, pltpu.VMEM) for x in inner))


def solution(mesh):
    tokens = P("dp", "ctx", None)
    return jax.shard_map(
        on_device,
        mesh=mesh,
        in_specs=(tokens, tokens, tokens, P(), tokens),
        out_specs=(tokens, tokens, tokens, tokens, P(("ctx", "dp"), None)),
        check_vma=False,
    )
```

```python
import functools
import math

import jax
import jax.numpy as jnp
from jax import lax
from jax.experimental import pallas as pl
from jax.experimental.pallas import tpu as pltpu
from jax.sharding import PartitionSpec as P

DK = 128
CH = 256
MESH = pl.DeviceIdType.MESH
BF = jnp.bfloat16
F32 = jnp.float32
PIECES = (
    (0, 384, "yxz", 0),
    (384, 384, "yzx", 1),
    (768, 384, "zxy", 0),
    (1152, 256, "zyx", 1),
    (1408, 384, "xyz", 0),
    (1792, 256, "xzy", 1),
)
AXES = "xzy"


def dot_nn(a, b):
    return lax.dot_general(a, b, (((1,), (0,)), ((), ())), preferred_element_type=F32)


def dot_nt(a, b):
    return lax.dot_general(a, b, (((1,), (1,)), ((), ())), preferred_element_type=F32)


def dot_tn(a, b):
    return lax.dot_general(a, b, (((0,), (0,)), ((), ())), preferred_element_type=F32)


def head_cols(h):
    return pl.ds(pl.multiple_of(h * DK, DK), DK)


def masked(product, query_rows):
    rows = lax.broadcasted_iota(jnp.int32, (CH, CH), 0)
    cols = lax.broadcasted_iota(jnp.int32, (CH, CH), 1)
    keep = rows >= cols if query_rows else rows <= cols
    return jnp.where(keep, product, 0.0).astype(BF)


def token_factor(me, shape, axis):
    pos = me * 512 + lax.broadcasted_iota(jnp.int32, shape, axis)
    return lax.rsqrt(((pos + 1) * DK).astype(F32))


def main_kernel(
    grad_scale,
    q_hbm, k_hbm, v_hbm, w_hbm, og_hbm,
    att, qg, kg, vg, wgrad,
    qb, kb, vb, wb, og_both, scaled, inner_t, att_full, at_both, weights_t,
    s1, g2, tx_kv, rx_kv, px_kv, before, tx_g, rx_g, px_g, after,
    prod, rx1, sum1, rx2, sum2, rx3, middle,
    in_sem, og_sem, kv1_s, kv1_r, kv2_s, kv2_r, g1_s, g1_r, g2_s, g2_r,
    mate_s, mate_r, rs_s, rs_r,
):
    me = lax.axis_index("ctx")
    dp = lax.axis_index("dp")
    place = {"x": me // 4, "z": me % 4, "y": dp // 2}
    core = dp % 2
    mate = (me, (dp // 2) * 2 + (1 - core))
    count = 16

    def axis_peer(axis, to):
        at = dict(place)
        at[axis] = to
        return (at["x"] * 4 + at["z"], at["y"] * 2 + core)

    def by_head(first, last, one):
        def several(n, carry):
            for m in range(2):
                one(first + 2 * n + m, carry)
            return carry

        lax.fori_loop(0, (last - first) // 2, several, 0)

    loads = [
        pltpu.make_async_copy(src.at[0], dst, in_sem.at[n])
        for n, (src, dst) in enumerate(((k_hbm, kb), (v_hbm, vb), (og_hbm, og_both.at[0:512]), (q_hbm, qb)))
    ]
    loads.append(pltpu.make_async_copy(w_hbm, wb, in_sem.at[4]))
    loads[0].start()
    loads[1].start()

    barrier = pltpu.get_barrier_semaphore()
    for offset in range(1, count):
        pl.semaphore_signal(
            barrier, inc=1, device_id=((me + offset) % count, dp), device_id_type=MESH
        )
    pl.semaphore_signal(barrier, inc=1, device_id=mate, device_id_type=MESH)
    for offset in (1, 3):
        pl.semaphore_signal(
            barrier, inc=1, device_id=axis_peer("y", (place["y"] + offset) % 4), device_id_type=MESH
        )

    loads[0].wait()
    loads[1].wait()
    loads[2].start()
    loads[4].start()
    loads[3].start()
    low, high = slice(0, CH), slice(CH, 2 * CH)

    def pair_at(j):
        return (me // 2 + 1 + j) % (count // 2)

    def kv_one(j, carry):
        j = pair_at(j)
        wide = pl.ds(pl.multiple_of(j * 256, 256), 256)
        first = dot_tn(vb[low, wide], kb[low, wide])
        both = first + dot_tn(vb[high, wide], kb[high, wide])
        for n in range(2):
            part = slice(n * DK, (n + 1) * DK)
            s1[2 * j + n] = first[part, part].astype(BF)
            tx_kv[2 * j + n] = both[part, part].astype(BF)
        return carry

    def arrival(src, dst, send, recv, other):
        return pltpu.make_async_remote_copy(
            src_ref=src.at[other], dst_ref=dst.at[other], send_sem=send.at[other],
            recv_sem=recv.at[other], device_id=(other, dp), device_id_type=MESH,
        )

    def send_one(src, dst, send, recv, other):
        @pl.when(other != me)
        def _():
            pltpu.make_async_remote_copy(
                src_ref=src.at[other], dst_ref=dst.at[me], send_sem=send.at[other],
                recv_sem=recv.at[me], device_id=(other, dp), device_id_type=MESH,
            ).start()

    def send_all(src, dst, send, recv):
        def one(n, carry):
            send_one(src, dst, send, recv, (me + n) % count)
            return carry

        lax.fori_loop(1, count, one, 0)

    def kv_send(j, carry):
        kv_one(j, carry)
        for n in range(2):
            send_one(tx_kv, rx_kv, kv1_s, kv1_r, 2 * pair_at(j) + n)
        return carry

    def kv_sent(j, carry):
        for n in range(2):
            send_one(tx_kv, rx_kv, kv1_s, kv1_r, 2 * pair_at(j) + n)
        return carry

    lax.fori_loop(0, count // 4, kv_one, 0)
    pl.semaphore_wait(barrier, count - 1 + 1 + 2)
    lax.fori_loop(0, count // 4, kv_sent, 0)
    lax.fori_loop(count // 4, count // 2, kv_send, 0)
    rx_kv[me] = tx_kv[me]

    loads[2].wait()
    og_copy = pltpu.make_async_remote_copy(
        src_ref=og_both.at[0:512], dst_ref=og_both.at[512:1024], send_sem=og_sem.at[0], recv_sem=og_sem.at[1],
        device_id=mate, device_id_type=MESH,
    )
    og_copy.start()

    def scan(src, dst, send, recv, src2, dst2, send2, recv2, reverse):
        def one(n, total):
            b = count - 1 - n if reverse else n

            @pl.when(b != me)
            def _():
                arrival(src, dst, send, recv, b).wait_recv()

            src2[b] = total.astype(BF)

            return total + dst[b].astype(F32)

        lax.fori_loop(0, count, one, jnp.zeros((DK, DK), F32))
        dst2[me] = src2[me]
        send_all(src2, dst2, send2, recv2)

    def finish(src, dst, send, recv, which):
        def one(offset, carry):
            other = (me + offset) % count
            if which == "recv":
                arrival(src, dst, send, recv, other).wait_recv()
            else:
                arrival(src, dst, send, recv, other).wait_send()
            return carry

        lax.fori_loop(1, count, one, 0)

    loads[4].wait()
    loads[3].wait()

    def grad_out_of(j):
        wide = pl.ds(pl.multiple_of(pair_at(j) * 256, 256), 256)
        grad_out = dot_nt(og_both[0:512], wb[wide, :]).astype(BF).astype(F32)
        scaled[:, wide] = (grad_out * token_factor(me, (512, 256), 0)).astype(BF)

    def grad_state_of(j):
        j = pair_at(j)
        wide = pl.ds(pl.multiple_of(j * 256, 256), 256)
        late = dot_tn(qb[high, wide], scaled[high, wide])
        both = late + dot_tn(qb[low, wide], scaled[low, wide])
        for n in range(2):
            part = slice(n * DK, (n + 1) * DK)
            g2[2 * j + n] = late[part, part].astype(BF)
            tx_g[2 * j + n] = both[part, part].astype(BF)

    def grad_one(j, carry):
        grad_state_of(j - 1)
        grad_out_of(j)
        return carry

    grad_out_of(0)
    lax.fori_loop(1, 6, grad_one, 0)
    scan(tx_kv, rx_kv, kv1_s, kv1_r, px_kv, before, kv2_s, kv2_r, False)
    lax.fori_loop(6, count // 2, grad_one, 0)
    grad_state_of(count // 2 - 1)
    rx_g[me] = tx_g[me]
    send_all(tx_g, rx_g, g1_s, g1_r)


    def inner_one(h, carry):
        cols = head_cols(h)
        turned = vb[:, cols].T
        for c, rows in enumerate((low, high)):
            weights_t[h, c] = masked(dot_nt(kb[rows, cols], qb[rows, cols]), False)
            part = dot_nn(turned[:, rows], weights_t[h, c])
            if c == 1:
                part = part + dot_nt(s1[h], qb[rows, cols])
            inner_t[h, :, rows] = part
        return carry

    by_head(0, count, inner_one)

    def mate_copy(h):
        return pltpu.make_async_remote_copy(
            src_ref=att_full.at[h, :, 1 - core], dst_ref=at_both.at[h, :, :, pl.ds(512, 512)], send_sem=mate_s.at[h],
            recv_sem=mate_r.at[h], device_id=mate, device_id_type=MESH,
        )

    def att_some(step, carry):
        heads = [(me + count - 2 * step - m) % count for m in range(2)]
        for m, h in enumerate(heads):

            @pl.when(2 * step + m > 0)
            def _(h=h):
                arrival(px_kv, before, kv2_s, kv2_r, h).wait_recv()

        factor = token_factor(me, (1, 512), 1)
        totals = [
            ((inner_t[h] + dot_nt(before[h], qb[:, head_cols(h)])) * factor).astype(BF)
            for h in heads
        ]
        for h, total in zip(heads, totals):
            att_full[h] = total.reshape(4, 2, 16, 512)
        for h in heads:
            at_both[h, :, :, 0:512] = att_full[h, :, core]
            mate_copy(h).start()
        return carry

    lax.fori_loop(0, count // 2, att_some, 0)
    scan(tx_g, rx_g, g1_s, g1_r, px_g, after, g2_s, g2_r, True)

    og_copy.wait()

    def mate_wait(h, carry):
        mate_copy(h).wait()
        return carry

    lax.fori_loop(0, count, mate_wait, 0)

    def pick(ref, axes, axis, t):
        index = tuple(t if a == axis else slice(None) for a in axes)
        return ref.at[index]

    def partners(p, c):
        pair = (c + 1 - 2 * (c % 2), 3 - c)
        return pair if PIECES[p][3] == 0 else pair[::-1]

    def rs_parts(p, phase):
        order = PIECES[p][2]
        axes = [a for a in AXES if a not in order[:phase]]
        axis = order[phase]
        return (prod, sum1, sum2)[phase][p], (rx1, rx2, rx3)[phase][p], axes, axis

    def rs_copy(p, phase, slot):
        src, dst, axes, axis = rs_parts(p, phase)
        one, two = partners(p, place[axis])
        if phase > 0:
            to = (place[axis] + slot + 1) % 4
            out = pick(src, axes, axis, to)
        elif slot == 0:
            out, to = pick(src, axes, axis, one), one
        elif slot == 1:
            out, to = pick(src, axes, axis, partners(p, one)[1]), one
        else:
            out, to = middle[p], two
        return pltpu.make_async_remote_copy(
            src_ref=out, dst_ref=dst.at[slot],
            send_sem=rs_s.at[phase, p, slot], recv_sem=rs_r.at[phase, p, slot],
            device_id=axis_peer(axis, to), device_id_type=MESH,
        )

    def rs_begin(p, phase):
        for slot in (1, 0) if phase == 0 else (0, 2, 1):
            rs_copy(p, phase, slot).start()

    def rs_mid(p):
        src, dst, axes, axis = rs_parts(p, 0)
        two = partners(p, place[axis])[1]
        rs_copy(p, 0, 1).wait_recv()
        total = pick(src, axes, axis, two)[...].astype(F32) + dst[1].astype(F32)
        middle[p][...] = total.astype(BF)
        rs_copy(p, 0, 2).start()

    def rs_sum(p, phase):
        src, dst, axes, axis = rs_parts(p, phase)
        slots = (0, 2) if phase == 0 else (0, 1, 2)
        for slot in slots:
            rs_copy(p, phase, slot).wait_recv()
        total = pick(src, axes, axis, place[axis])[...].astype(F32)
        for slot in slots:
            total = total + dst[slot].astype(F32)
        return total

    for p, (first, width, _, _) in enumerate(PIECES):
        left = at_both[...].reshape(1024, 1024)
        part = dot_nn(left, og_both[:, first : first + width])
        prod[p][...] = part.astype(BF).reshape(4, 4, 4, 16, width)
        rs_begin(p, 0)

    def query_one(h, carry):
        cols = head_cols(h)
        att[:, cols] = att_full[h].reshape(DK, 512).T
        before_of = (before[h], (before[h].astype(F32) + s1[h].astype(F32)).astype(BF))
        for c, rows in enumerate((low, high)):
            kc, vc, sc = kb[rows, cols], vb[rows, cols], scaled[rows, cols]
            mixing = masked(dot_nt(sc, vc), True)
            query_grad = dot_nn(mixing, kc) + dot_nn(sc, before_of[c])
            qg[rows, cols] = query_grad.astype(BF)
        return carry

    def key_one(h, carry):
        cols = head_cols(h)
        after_of = ((after[h].astype(F32) + g2[h].astype(F32)).astype(BF), after[h])
        for c, rows in enumerate((low, high)):
            qc, kc, vc, sc = qb[rows, cols], kb[rows, cols], vb[rows, cols], scaled[rows, cols]
            mixing_t = masked(dot_nt(vc, sc), False)
            key_grad = dot_nn(mixing_t, qc) + dot_nt(vc, after_of[c])
            value_grad = dot_nn(weights_t[h, c], sc) + dot_nn(kc, after_of[c])
            kg[rows, cols] = key_grad.astype(BF)
            vg[rows, cols] = value_grad.astype(BF)
        return carry

    def next_phase(phase):
        for p in range(len(PIECES)):
            (sum1, sum2)[phase - 1][p][...] = rs_sum(p, phase - 1).astype(BF)
            rs_begin(p, phase)

    by_head(0, count, query_one)
    for p in range(len(PIECES)):
        rs_mid(p)
    next_phase(1)
    finish(px_g, after, g2_s, g2_r, "recv")
    by_head(0, 10, key_one)
    next_phase(2)
    by_head(10, 16, key_one)
    for p, (first, width, _, _) in enumerate(PIECES):
        wgrad[:, first : first + width] = rs_sum(p, 2) * grad_scale
    finish(tx_kv, rx_kv, kv1_s, kv1_r, "send")
    finish(tx_g, rx_g, g1_s, g1_r, "send")
    finish(px_kv, before, kv2_s, kv2_r, "send")
    finish(px_g, after, g2_s, g2_r, "send")
    for p in range(len(PIECES)):
        for phase in range(3):
            for slot in range(3):
                rs_copy(p, phase, slot).wait_send()

def main_call(q, k, v, w, og, grad_scale):
    any_spec = pl.BlockSpec(memory_space=pl.ANY)
    n = len(PIECES)
    widths = [width for _, width, _, _ in PIECES]
    vm = pltpu.VMEM
    sem = pltpu.SemaphoreType.DMA
    state = vm((16, DK, DK), BF)
    scratch = [
        vm((512, 2048), BF), vm((512, 2048), BF), vm((512, 2048), BF), vm((2048, 2048), BF),
        vm((1024, 2048), BF), vm((512, 2048), BF), vm((16, DK, 512), F32),
        vm((16, 4, 2, 16, 512), BF), vm((16, 4, 16, 1024), BF), vm((16, 2, CH, CH), BF),
        state, state, state, state, state, state, state, state, state, state,
        [vm((4, 4, 4, 16, c), BF) for c in widths],
        [vm((3, 4, 4, 16, c), BF) for c in widths],
        [vm((4, 4, 16, c), BF) for c in widths],
        [vm((3, 4, 16, c), BF) for c in widths],
        [vm((4, 16, c), BF) for c in widths],
        [vm((3, 16, c), BF) for c in widths],
        [vm((4, 4, 16, c), BF) for c in widths],
        sem((5,)), sem((2,)),
        sem((16,)), sem((16,)), sem((16,)), sem((16,)),
        sem((16,)), sem((16,)), sem((16,)), sem((16,)),
        sem((16,)), sem((16,)), sem((3, n, 3)), sem((3, n, 3)),
    ]
    return pl.pallas_call(
        functools.partial(main_kernel, grad_scale),
        out_shape=(vm((512, 2048), BF),) * 4 + (vm((16, 2048), F32),),
        in_specs=[any_spec] * 5,
        out_specs=(pl.BlockSpec(memory_space=vm),) * 5,
        scratch_shapes=scratch,
        compiler_params=pltpu.CompilerParams(
            collective_id=1, has_side_effects=True, vmem_limit_bytes=52 << 20
        ),
        name="states_and_weight_grad",
    )(q, k, v, w, og)


def place_kernel(*refs):
    sem = refs[-1]
    copies = []
    for n in range(4):
        for half in range(2):
            rows = pl.ds(half * 256, 256)
            copies.append(
                pltpu.make_async_copy(
                    refs[n].at[rows], refs[5 + n].at[0, rows], sem.at[2 * n + half]
                )
            )
    copies.append(pltpu.make_async_copy(refs[4], refs[9], sem.at[8]))
    for copy in copies:
        copy.start()
    for copy in copies:
        copy.wait()


def place_call(*arrays):
    any_spec = pl.BlockSpec(memory_space=pl.ANY)
    return pl.pallas_call(
        place_kernel,
        out_shape=(jax.ShapeDtypeStruct((1, 512, 2048), BF),) * 4
        + (jax.ShapeDtypeStruct((16, 2048), F32),),
        in_specs=[pl.BlockSpec(memory_space=pltpu.VMEM)] * 5,
        out_specs=(any_spec,) * 5,
        scratch_shapes=[pltpu.SemaphoreType.DMA((9,))],
        compiler_params=pltpu.CompilerParams(vmem_limit_bytes=2 << 20),
        name="place_outputs",
    )(*arrays)


def on_device(queries, keys, values, out_weight, out_grad):
    grad_scale = 1.0 / math.sqrt(8 * 8192)
    inner = main_call(queries, keys, values, out_weight, out_grad, grad_scale)
    return place_call(*(pltpu.with_memory_space_constraint(x, pltpu.VMEM) for x in inner))


def solution(mesh):
    tokens = P("dp", "ctx", None)
    return jax.shard_map(
        on_device,
        mesh=mesh,
        in_specs=(tokens, tokens, tokens, P(), tokens),
        out_specs=(tokens, tokens, tokens, tokens, P(("ctx", "dp"), None)),
        check_vma=False,
    )
```

```python
import functools
import math

import jax
import jax.numpy as jnp
from jax import lax
from jax.experimental import pallas as pl
from jax.experimental.pallas import tpu as pltpu
from jax.sharding import PartitionSpec as P

DK = 128
CH = 256
MESH = pl.DeviceIdType.MESH
BF = jnp.bfloat16
F32 = jnp.float32
PIECES = (
    (0, 384, "yxz", 0),
    (384, 384, "yzx", 1),
    (768, 384, "zxy", 0),
    (1152, 256, "zyx", 1),
    (1408, 384, "xyz", 0),
    (1792, 256, "xzy", 1),
)
AXES = "xzy"


def dot_nn(a, b):
    return lax.dot_general(a, b, (((1,), (0,)), ((), ())), preferred_element_type=F32)


def dot_nt(a, b):
    return lax.dot_general(a, b, (((1,), (1,)), ((), ())), preferred_element_type=F32)


def dot_tn(a, b):
    return lax.dot_general(a, b, (((0,), (0,)), ((), ())), preferred_element_type=F32)


def head_cols(h):
    return pl.ds(pl.multiple_of(h * DK, DK), DK)


def masked(product, query_rows):
    rows = lax.broadcasted_iota(jnp.int32, (CH, CH), 0)
    cols = lax.broadcasted_iota(jnp.int32, (CH, CH), 1)
    keep = rows >= cols if query_rows else rows <= cols
    return jnp.where(keep, product, 0.0).astype(BF)


def token_factor(me, shape, axis):
    pos = me * 512 + lax.broadcasted_iota(jnp.int32, shape, axis)
    return lax.rsqrt(((pos + 1) * DK).astype(F32))


def main_kernel(
    grad_scale,
    q_hbm, k_hbm, v_hbm, w_hbm, og_hbm,
    att, qg, kg, vg, wgrad,
    qb, kb, vb, wb, og_both, scaled, inner_t, att_full, at_both, weights_t,
    s1, g2, tx_kv, rx_kv, px_kv, before, tx_g, rx_g, px_g, after,
    prod, rx1, sum1, rx2, sum2, rx3, middle,
    in_sem, og_sem, kv1_s, kv1_r, kv2_s, kv2_r, g1_s, g1_r, g2_s, g2_r,
    mate_s, mate_r, rs_s, rs_r,
):
    me = lax.axis_index("ctx")
    dp = lax.axis_index("dp")
    place = {"x": me // 4, "z": me % 4, "y": dp // 2}
    core = dp % 2
    mate = (me, (dp // 2) * 2 + (1 - core))
    count = 16

    def axis_peer(axis, to):
        at = dict(place)
        at[axis] = to
        return (at["x"] * 4 + at["z"], at["y"] * 2 + core)

    def by_head(first, last, one):
        def several(n, carry):
            for m in range(2):
                one(first + 2 * n + m, carry)
            return carry

        lax.fori_loop(0, (last - first) // 2, several, 0)

    loads = [
        pltpu.make_async_copy(src.at[0], dst, in_sem.at[n])
        for n, (src, dst) in enumerate(((k_hbm, kb), (v_hbm, vb), (og_hbm, og_both.at[0:512]), (q_hbm, qb)))
    ]
    loads.append(pltpu.make_async_copy(w_hbm, wb, in_sem.at[4]))
    loads[0].start()
    loads[1].start()

    barrier = pltpu.get_barrier_semaphore()
    for offset in range(1, count):
        pl.semaphore_signal(
            barrier, inc=1, device_id=((me + offset) % count, dp), device_id_type=MESH
        )
    pl.semaphore_signal(barrier, inc=1, device_id=mate, device_id_type=MESH)
    for offset in (1, 3):
        pl.semaphore_signal(
            barrier, inc=1, device_id=axis_peer("y", (place["y"] + offset) % 4), device_id_type=MESH
        )

    loads[0].wait()
    loads[1].wait()
    loads[2].start()
    loads[4].start()
    loads[3].start()
    low, high = slice(0, CH), slice(CH, 2 * CH)

    def pair_at(j):
        return (me // 2 + 1 + j) % (count // 2)

    def kv_one(j, carry):
        j = pair_at(j)
        wide = pl.ds(pl.multiple_of(j * 256, 256), 256)
        first = dot_tn(vb[low, wide], kb[low, wide])
        both = first + dot_tn(vb[high, wide], kb[high, wide])
        for n in range(2):
            part = slice(n * DK, (n + 1) * DK)
            s1[2 * j + n] = first[part, part].astype(BF)
            tx_kv[2 * j + n] = both[part, part].astype(BF)
        return carry

    def arrival(src, dst, send, recv, other):
        return pltpu.make_async_remote_copy(
            src_ref=src.at[other], dst_ref=dst.at[other], send_sem=send.at[other],
            recv_sem=recv.at[other], device_id=(other, dp), device_id_type=MESH,
        )

    def send_one(src, dst, send, recv, other):
        @pl.when(other != me)
        def _():
            pltpu.make_async_remote_copy(
                src_ref=src.at[other], dst_ref=dst.at[me], send_sem=send.at[other],
                recv_sem=recv.at[me], device_id=(other, dp), device_id_type=MESH,
            ).start()

    def send_all(src, dst, send, recv):
        def one(n, carry):
            send_one(src, dst, send, recv, (me + n) % count)
            return carry

        lax.fori_loop(1, count, one, 0)

    def kv_send(j, carry):
        kv_one(j, carry)
        for n in range(2):
            send_one(tx_kv, rx_kv, kv1_s, kv1_r, 2 * pair_at(j) + n)
        return carry

    def kv_sent(j, carry):
        for n in range(2):
            send_one(tx_kv, rx_kv, kv1_s, kv1_r, 2 * pair_at(j) + n)
        return carry

    lax.fori_loop(0, count // 4, kv_one, 0)
    pl.semaphore_wait(barrier, count - 1 + 1 + 2)
    lax.fori_loop(0, count // 4, kv_sent, 0)
    lax.fori_loop(count // 4, count // 2, kv_send, 0)
    rx_kv[me] = tx_kv[me]

    loads[2].wait()
    og_copy = pltpu.make_async_remote_copy(
        src_ref=og_both.at[0:512], dst_ref=og_both.at[512:1024], send_sem=og_sem.at[0], recv_sem=og_sem.at[1],
        device_id=mate, device_id_type=MESH,
    )
    og_copy.start()

    def scan(src, dst, send, recv, src2, dst2, send2, recv2, reverse):
        def one(n, total):
            b = count - 1 - n if reverse else n

            @pl.when(b != me)
            def _():
                arrival(src, dst, send, recv, b).wait_recv()

            src2[b] = total.astype(BF)

            return total + dst[b].astype(F32)

        lax.fori_loop(0, count, one, jnp.zeros((DK, DK), F32))
        dst2[me] = src2[me]
        send_all(src2, dst2, send2, recv2)

    def finish(src, dst, send, recv, which):
        def one(offset, carry):
            other = (me + offset) % count
            if which == "recv":
                arrival(src, dst, send, recv, other).wait_recv()
            else:
                arrival(src, dst, send, recv, other).wait_send()
            return carry

        lax.fori_loop(1, count, one, 0)

    loads[4].wait()
    loads[3].wait()

    def grad_out_of(j):
        wide = pl.ds(pl.multiple_of(pair_at(j) * 256, 256), 256)
        grad_out = dot_nt(og_both[0:512], wb[wide, :]).astype(BF).astype(F32)
        scaled[:, wide] = (grad_out * token_factor(me, (512, 256), 0)).astype(BF)

    def grad_state_of(j):
        j = pair_at(j)
        wide = pl.ds(pl.multiple_of(j * 256, 256), 256)
        late = dot_tn(qb[high, wide], scaled[high, wide])
        both = late + dot_tn(qb[low, wide], scaled[low, wide])
        for n in range(2):
            part = slice(n * DK, (n + 1) * DK)
            g2[2 * j + n] = late[part, part].astype(BF)
            tx_g[2 * j + n] = both[part, part].astype(BF)

    def grad_one(j, carry):
        grad_state_of(j - 1)
        grad_out_of(j)
        return carry

    grad_out_of(0)
    lax.fori_loop(1, 6, grad_one, 0)
    scan(tx_kv, rx_kv, kv1_s, kv1_r, px_kv, before, kv2_s, kv2_r, False)
    lax.fori_loop(6, count // 2, grad_one, 0)
    grad_state_of(count // 2 - 1)
    rx_g[me] = tx_g[me]
    send_all(tx_g, rx_g, g1_s, g1_r)


    def inner_one(h, carry):
        cols = head_cols(h)
        turned = vb[:, cols].T
        for c, rows in enumerate((low, high)):
            weights_t[h, c] = masked(dot_nt(kb[rows, cols], qb[rows, cols]), False)
            part = dot_nn(turned[:, rows], weights_t[h, c])
            if c == 1:
                part = part + dot_nt(s1[h], qb[rows, cols])
            inner_t[h, :, rows] = part
        return carry

    by_head(0, count, inner_one)

    def mate_copy(h):
        return pltpu.make_async_remote_copy(
            src_ref=att_full.at[h, :, 1 - core], dst_ref=at_both.at[h, :, :, pl.ds(512, 512)], send_sem=mate_s.at[h],
            recv_sem=mate_r.at[h], device_id=mate, device_id_type=MESH,
        )

    def att_some(step, carry):
        heads = [(me + count - 2 * step - m) % count for m in range(2)]
        for m, h in enumerate(heads):

            @pl.when(2 * step + m > 0)
            def _(h=h):
                arrival(px_kv, before, kv2_s, kv2_r, h).wait_recv()

        factor = token_factor(me, (1, 512), 1)
        totals = [
            ((inner_t[h] + dot_nt(before[h], qb[:, head_cols(h)])) * factor).astype(BF)
            for h in heads
        ]
        for h, total in zip(heads, totals):
            att_full[h] = total.reshape(4, 2, 16, 512)
        for h in heads:
            at_both[h, :, :, 0:512] = att_full[h, :, core]
            mate_copy(h).start()
        return carry

    lax.fori_loop(0, count // 2, att_some, 0)
    scan(tx_g, rx_g, g1_s, g1_r, px_g, after, g2_s, g2_r, True)

    og_copy.wait()

    def mate_wait(h, carry):
        mate_copy(h).wait()
        return carry

    lax.fori_loop(0, count, mate_wait, 0)

    def pick(ref, axes, axis, t):
        index = tuple(t if a == axis else slice(None) for a in axes)
        return ref.at[index]

    def partners(p, c):
        pair = (c + 1 - 2 * (c % 2), 3 - c)
        return pair if PIECES[p][3] == 0 else pair[::-1]

    def rs_parts(p, phase):
        order = PIECES[p][2]
        axes = [a for a in AXES if a not in order[:phase]]
        axis = order[phase]
        return (prod, sum1, sum2)[phase][p], (rx1, rx2, rx3)[phase][p], axes, axis

    def rs_copy(p, phase, slot):
        src, dst, axes, axis = rs_parts(p, phase)
        one, two = partners(p, place[axis])
        if phase > 0:
            to = (place[axis] + slot + 1) % 4
            out = pick(src, axes, axis, to)
        elif slot == 0:
            out, to = pick(src, axes, axis, one), one
        elif slot == 1:
            out, to = pick(src, axes, axis, partners(p, one)[1]), one
        else:
            out, to = middle[p], two
        return pltpu.make_async_remote_copy(
            src_ref=out, dst_ref=dst.at[slot],
            send_sem=rs_s.at[phase, p, slot], recv_sem=rs_r.at[phase, p, slot],
            device_id=axis_peer(axis, to), device_id_type=MESH,
        )

    def rs_begin(p, phase):
        for slot in (0, 2, 1):
            rs_copy(p, phase, slot).start()

    def rs_mid(p):
        src, dst, axes, axis = rs_parts(p, 0)
        two = partners(p, place[axis])[1]
        rs_copy(p, 0, 1).wait_recv()
        total = pick(src, axes, axis, two)[...].astype(F32) + dst[1].astype(F32)
        middle[p][...] = total.astype(BF)
        rs_copy(p, 0, 2).start()

    def rs_sum(p, phase):
        src, dst, axes, axis = rs_parts(p, phase)
        slots = (0, 2) if phase == 0 else (0, 1, 2)
        for slot in slots:
            rs_copy(p, phase, slot).wait_recv()
        total = pick(src, axes, axis, place[axis])[...].astype(F32)
        for slot in slots:
            total = total + dst[slot].astype(F32)
        return total

    for p, (first, width, _, _) in enumerate(PIECES):
        left = at_both[...].reshape(1024, 1024)
        part = dot_nn(left, og_both[:, first : first + width])
        prod[p][...] = part.astype(BF).reshape(4, 4, 4, 16, width)
        rs_copy(p, 0, 1).start()

    for p in range(len(PIECES)):
        rs_copy(p, 0, 0).start()

    def query_one(h, carry):
        cols = head_cols(h)
        att[:, cols] = att_full[h].reshape(DK, 512).T
        before_of = (before[h], (before[h].astype(F32) + s1[h].astype(F32)).astype(BF))
        for c, rows in enumerate((low, high)):
            kc, vc, sc = kb[rows, cols], vb[rows, cols], scaled[rows, cols]
            mixing = masked(dot_nt(sc, vc), True)
            query_grad = dot_nn(mixing, kc) + dot_nn(sc, before_of[c])
            qg[rows, cols] = query_grad.astype(BF)
        return carry

    def key_one(h, carry):
        cols = head_cols(h)
        after_of = ((after[h].astype(F32) + g2[h].astype(F32)).astype(BF), after[h])
        for c, rows in enumerate((low, high)):
            qc, kc, vc, sc = qb[rows, cols], kb[rows, cols], vb[rows, cols], scaled[rows, cols]
            mixing_t = masked(dot_nt(vc, sc), False)
            key_grad = dot_nn(mixing_t, qc) + dot_nt(vc, after_of[c])
            value_grad = dot_nn(weights_t[h, c], sc) + dot_nn(kc, after_of[c])
            kg[rows, cols] = key_grad.astype(BF)
            vg[rows, cols] = value_grad.astype(BF)
        return carry

    def next_phase(phase):
        for p in range(len(PIECES)):
            (sum1, sum2)[phase - 1][p][...] = rs_sum(p, phase - 1).astype(BF)
            rs_begin(p, phase)

    by_head(0, 8, query_one)
    for p in (0, 1):
        rs_mid(p)
    by_head(8, 12, query_one)
    for p in (2, 3):
        rs_mid(p)
    by_head(12, count, query_one)
    for p in (4, 5):
        rs_mid(p)
    next_phase(1)
    finish(px_g, after, g2_s, g2_r, "recv")
    by_head(0, 10, key_one)
    next_phase(2)
    by_head(10, 16, key_one)
    for p, (first, width, _, _) in enumerate(PIECES):
        wgrad[:, first : first + width] = rs_sum(p, 2) * grad_scale
    finish(tx_kv, rx_kv, kv1_s, kv1_r, "send")
    finish(tx_g, rx_g, g1_s, g1_r, "send")
    finish(px_kv, before, kv2_s, kv2_r, "send")
    finish(px_g, after, g2_s, g2_r, "send")
    for p in range(len(PIECES)):
        for phase in range(3):
            for slot in range(3):
                rs_copy(p, phase, slot).wait_send()

def main_call(q, k, v, w, og, grad_scale):
    any_spec = pl.BlockSpec(memory_space=pl.ANY)
    n = len(PIECES)
    widths = [width for _, width, _, _ in PIECES]
    vm = pltpu.VMEM
    sem = pltpu.SemaphoreType.DMA
    state = vm((16, DK, DK), BF)
    scratch = [
        vm((512, 2048), BF), vm((512, 2048), BF), vm((512, 2048), BF), vm((2048, 2048), BF),
        vm((1024, 2048), BF), vm((512, 2048), BF), vm((16, DK, 512), F32),
        vm((16, 4, 2, 16, 512), BF), vm((16, 4, 16, 1024), BF), vm((16, 2, CH, CH), BF),
        state, state, state, state, state, state, state, state, state, state,
        [vm((4, 4, 4, 16, c), BF) for c in widths],
        [vm((3, 4, 4, 16, c), BF) for c in widths],
        [vm((4, 4, 16, c), BF) for c in widths],
        [vm((3, 4, 16, c), BF) for c in widths],
        [vm((4, 16, c), BF) for c in widths],
        [vm((3, 16, c), BF) for c in widths],
        [vm((4, 4, 16, c), BF) for c in widths],
        sem((5,)), sem((2,)),
        sem((16,)), sem((16,)), sem((16,)), sem((16,)),
        sem((16,)), sem((16,)), sem((16,)), sem((16,)),
        sem((16,)), sem((16,)), sem((3, n, 3)), sem((3, n, 3)),
    ]
    return pl.pallas_call(
        functools.partial(main_kernel, grad_scale),
        out_shape=(vm((512, 2048), BF),) * 4 + (vm((16, 2048), F32),),
        in_specs=[any_spec] * 5,
        out_specs=(pl.BlockSpec(memory_space=vm),) * 5,
        scratch_shapes=scratch,
        compiler_params=pltpu.CompilerParams(
            collective_id=1, has_side_effects=True, vmem_limit_bytes=52 << 20
        ),
        name="states_and_weight_grad",
    )(q, k, v, w, og)


def place_kernel(*refs):
    sem = refs[-1]
    copies = []
    for n in range(4):
        for half in range(2):
            rows = pl.ds(half * 256, 256)
            copies.append(
                pltpu.make_async_copy(
                    refs[n].at[rows], refs[5 + n].at[0, rows], sem.at[2 * n + half]
                )
            )
    copies.append(pltpu.make_async_copy(refs[4], refs[9], sem.at[8]))
    for copy in copies:
        copy.start()
    for copy in copies:
        copy.wait()


def place_call(*arrays):
    any_spec = pl.BlockSpec(memory_space=pl.ANY)
    return pl.pallas_call(
        place_kernel,
        out_shape=(jax.ShapeDtypeStruct((1, 512, 2048), BF),) * 4
        + (jax.ShapeDtypeStruct((16, 2048), F32),),
        in_specs=[pl.BlockSpec(memory_space=pltpu.VMEM)] * 5,
        out_specs=(any_spec,) * 5,
        scratch_shapes=[pltpu.SemaphoreType.DMA((9,))],
        compiler_params=pltpu.CompilerParams(vmem_limit_bytes=2 << 20),
        name="place_outputs",
    )(*arrays)


def on_device(queries, keys, values, out_weight, out_grad):
    grad_scale = 1.0 / math.sqrt(8 * 8192)
    inner = main_call(queries, keys, values, out_weight, out_grad, grad_scale)
    return place_call(*(pltpu.with_memory_space_constraint(x, pltpu.VMEM) for x in inner))


def solution(mesh):
    tokens = P("dp", "ctx", None)
    return jax.shard_map(
        on_device,
        mesh=mesh,
        in_specs=(tokens, tokens, tokens, P(), tokens),
        out_specs=(tokens, tokens, tokens, tokens, P(("ctx", "dp"), None)),
        check_vma=False,
    )
```
